256 devices in a mesh: row: 32 (over y, z_lo, x), col: 8 (over z_hi, core).
Axes of the slice: x: 4, y: 4, z: 8 (z_hi: 4, z_lo: 2; z = z_hi * 2 + z_lo), core: 2. Of those that a mesh axis runs over, the one named last changes fastest.
Arguments:
- velocity: float32 [3, 32, 256, 4096], P(None, 'col', 'row'), may hold values from -14.4 to 14.4
Outputs:
- leonard: float32 [6, 32, 256, 4096], P(None, 'col', 'row')
- model: float32 [6, 32, 256, 4096], P(None, 'col', 'row')
- stress: float32 [6, 32, 256, 4096], P(None, 'col', 'row')
The draws below stay inside these ranges and needn't reach their ends.
All inputs are finite; a program needn't handle non-finite values.
Results may differ from the reference program's by a relative error of at most 0.00011.
Values sent between devices are 32-bit elements; how exact they have to be, the bound alone decides.
A program may use at most 320 MiB of HBM per device.

```python
import jax
import jax.numpy as jnp
from jax import lax

NX = 4096
NY = 256
NZ = 32


def draw_velocity(key, part):
    key = jax.random.fold_in(key, 11)
    first, second, third = jax.random.split(key, 3)
    shape = (3, NZ, NY, NX)
    base = jnp.clip(jax.random.normal(first, shape, jnp.float32), -4.0, 4.0)
    ramp = 0.6 + 1.2 * jnp.arange(NZ, dtype=jnp.float32) / max(NZ - 1, 1)
    plane_scale = ramp * jnp.exp(jax.random.uniform(second, (NZ,), jnp.float32, -0.223, 0.223))
    column_scale = jnp.exp(jax.random.uniform(third, (NX,), jnp.float32, -0.693, 0.47))
    return (base * plane_scale[None, :, None, None] * column_scale[None, None, None, :]).astype(jnp.float32)


def setup_inputs(seed: int = 0) -> dict:
    key_of = jax.random.split(jax.random.key(seed), 2)
    velocity = draw_velocity(jax.random.fold_in(key_of[1], 71), 0)
    return {"velocity": velocity}


pair_list = ((0, 0), (0, 1), (0, 2), (1, 1), (1, 2), (2, 2))
pair_weight = (1.0, 2.0, 2.0, 1.0, 2.0, 1.0)
filter_taps = (1.0 / 25, 2.0 / 25, 3.0 / 25, 4.0 / 25, 5.0 / 25, 4.0 / 25, 3.0 / 25, 2.0 / 25, 1.0 / 25)

def diff_x(field):
    return (jnp.roll(field, -1, -1) - jnp.roll(field, 1, -1)) * 0.5

def diff_y(field):
    padded = jnp.pad(field, ((0, 0), (1, 1), (0, 0)))
    return (padded[:, 2:, :] - padded[:, :-2, :]) * 0.5

def diff_z(field):
    padded = jnp.pad(field, ((1, 1), (0, 0), (0, 0)))
    return (padded[2:, :, :] - padded[:-2, :, :]) * 0.5

def strain_parts(vel):
    grads = [[diff_x(vel[i]), diff_y(vel[i]), diff_z(vel[i])] for i in range(3)]
    strain = [0.5 * (grads[i][j] + grads[j][i]) for i, j in pair_list]
    total = jnp.zeros_like(strain[0])
    for index in range(6):
        total = total + pair_weight[index] * strain[index] * strain[index]
    return (strain, jnp.sqrt(2.0 * total))

def test_filter(field):
    result = jnp.zeros_like(field)
    for k in range(9):
        result = result + filter_taps[k] * jnp.roll(field, 4 - k, -1)
    size_y = field.shape[1]
    padded = jnp.pad(result, ((0, 0), (4, 4), (0, 0)))
    result = jnp.zeros_like(field)
    for k in range(9):
        result = result + filter_taps[k] * padded[:, k:k + size_y, :]
    size_z = field.shape[0]
    padded = jnp.pad(result, ((4, 4), (0, 0), (0, 0)))
    result = jnp.zeros_like(field)
    for k in range(9):
        result = result + filter_taps[k] * padded[k:k + size_z, :, :]
    return result

def reference(velocity):
    strain, magnitude = strain_parts(velocity)
    bar_vel = [test_filter(velocity[i]) for i in range(3)]
    leonard = []
    for i, j in pair_list:
        leonard.append(test_filter(velocity[i] * velocity[j]) - bar_vel[i] * bar_vel[j])
    bar_strain, bar_mag = strain_parts(jnp.stack(bar_vel))
    model = []
    for index in range(6):
        smoothed = test_filter(magnitude * strain[index])
        model.append(2.0 * (smoothed - 4.0 * bar_mag * bar_strain[index]))
    numer = jnp.zeros((velocity.shape[2],), jnp.float32)
    denom = jnp.zeros((velocity.shape[2],), jnp.float32)
    for index in range(6):
        numer = numer + lax.optimization_barrier(jnp.sum(pair_weight[index] * leonard[index] * model[index], axis=(0, 2)))
        denom = denom + lax.optimization_barrier(jnp.sum(pair_weight[index] * model[index] * model[index], axis=(0, 2)))
    count = velocity.shape[1] * velocity.shape[3]
    coeff = jnp.maximum(numer / count / (denom / count + 1e-06), 0.0)
    stress = [-2.0 * coeff[None, :, None] * magnitude * strain[index] for index in range(6)]
    return (jnp.stack(leonard), jnp.stack(model), jnp.stack(stress))
```

```python
import functools

import jax
import jax.numpy as jnp
import numpy as np
from jax import lax
from jax.experimental import pallas as pl
from jax.experimental.pallas import tpu as pltpu
from jax.sharding import PartitionSpec as P

MESH = pl.DeviceIdType.MESH
HBM = pltpu.MemorySpace.HBM
VMEM = pltpu.MemorySpace.VMEM
pair_list = ((0, 0), (0, 1), (0, 2), (1, 1), (1, 2), (2, 2))
pair_weight = (1.0, 2.0, 2.0, 1.0, 2.0, 1.0)

DZ = 4
DY = 8
H = 5
EZ = DZ + 2 * H
EY = DY + 2 * H
VMEM_LIMIT = 60 * 1024 * 1024


def shifted(u, by):
    nt = u.shape[0]
    lane = lax.broadcasted_iota(jnp.int32, u.shape, 1)
    if by == 1:
        near = pltpu.roll(u, 127, 1)
        return jnp.where(lane == 127, pltpu.roll(near, nt - 1, 0), near)
    near = pltpu.roll(u, 1, 1)
    return jnp.where(lane == 0, pltpu.roll(near, 1, 0), near)


def double_box(cells):
    for _ in range(2):
        two = [a + b for a, b in zip(cells, cells[1:])]
        four = [a + b for a, b in zip(two, two[2:])]
        cells = [a + b for a, b in zip(four, cells[4:])]
    return cells


def strain_scaled(grads):
    diag = [grads[i][i] for i in range(3)]
    off = [grads[i][j] + grads[j][i] for i, j in ((0, 1), (0, 2), (1, 2))]
    total = 2.0 * (diag[0] * diag[0] + diag[1] * diag[1] + diag[2] * diag[2])
    total = total + (off[0] * off[0] + off[1] * off[1] + off[2] * off[2])
    quarter = jnp.sqrt(total * (1.0 / 64.0))
    diag = [d + d for d in diag]
    return (diag[0], off[0], off[1], diag[1], off[2], diag[2]), quarter


def halo_kernel(rows, cols, nt, vel, fp, fv, ms, e, t, zp, zv, z_send, z_recv, y_send, y_recv, s_send, s_recv):
    r = lax.axis_index("row")
    c = lax.axis_index("col")
    odd = lax.rem(c, 2)
    out = 2 * odd - 1
    sibling = c - out
    outer1, outer2, inner2 = c + out, c + 2 * out, c - 2 * out
    has_outer = jnp.logical_and(outer1 >= 0, outer1 < cols)
    has_inner2 = jnp.logical_and(inner2 >= 0, inner2 < cols)
    has_up = r > 0
    has_down = r < rows - 1

    barrier = pltpu.get_barrier_semaphore()
    partners = (
        (has_up, r - 1, c),
        (has_down, r + 1, c),
        (c >= 0, r, sibling),
        (has_outer, r, outer1),
        (has_outer, r, outer2),
        (has_inner2, r, inner2),
    )
    count = 0
    for there, row, col in partners:

        @pl.when(there)
        def _(row=row, col=col):
            pl.semaphore_signal(barrier, inc=1, device_id=(row, col), device_id_type=MESH)

        count = count + there.astype(jnp.int32)

    @pl.loop(0, 3 * DZ)
    def _(n):
        i, k = n // DZ, lax.rem(n, DZ)
        for x in range(nt):
            e[i, H + k, pl.ds(H * nt + x, DY, stride=nt), :] = vel[i, k, :, x * 128 : (x + 1) * 128]

    def line(q, start=0, size=nt):
        return pl.ds(pl.multiple_of(q * nt + start, 8), size)

    zero = jnp.zeros((nt, 128), jnp.float32)
    mine = H * odd

    def clear(plane0, planes, row0, count_rows):
        @pl.loop(0, 3 * planes * count_rows)
        def _(n):
            i, rest = n // (planes * count_rows), lax.rem(n, planes * count_rows)
            e[i, plane0 + rest // count_rows, line(row0 + lax.rem(rest, count_rows)), :] = zero

    @pl.when(jnp.logical_not(has_up))
    def _():
        clear(mine, EZ - H, 0, H)

    @pl.when(jnp.logical_not(has_down))
    def _():
        clear(mine, EZ - H, H + DY, H)

    @pl.when(jnp.logical_not(has_outer))
    def _():
        clear(odd * (H + DZ), H, 0, EY)

    pl.semaphore_wait(barrier, count)

    def copy(p_src, p_dst, planes, q_src, q_dst, count_rows, send, recv, row, col):
        return pltpu.make_async_remote_copy(
            src_ref=e.at[:, pl.ds(p_src, planes), pl.ds(q_src * nt, count_rows * nt)],
            dst_ref=e.at[:, pl.ds(p_dst, planes), pl.ds(q_dst * nt, count_rows * nt)],
            send_sem=send,
            recv_sem=recv,
            device_id=(row, col),
            device_id_type=MESH,
        )

    own = H
    outer_plane = [4 - j + odd * (5 + 2 * j) for j in range(H)]

    def z_copy(j):
        if j < 4:
            k = j + odd * (3 - 2 * j)
            dst = 9 + j - odd * (5 + 2 * j)
            return copy(own + k, dst, 1, H, H, DY, z_send.at[j], z_recv.at[j], r, outer1)
        return copy(8 - 3 * odd, 13 * odd, 1, H, H, DY, z_send.at[4], z_recv.at[4], r, inner2)

    def y_copies(n):
        plane, planes = (own, DZ) if n == 0 else (outer_plane[n - 1], 1)
        up = copy(plane, plane, planes, H, H + DY, H, y_send.at[0, n], y_recv.at[0, n], r - 1, c)
        down = copy(plane, plane, planes, DY, 0, H, y_send.at[1, n], y_recv.at[1, n], r + 1, c)
        return up, down

    def s_copy(n):
        dst = 1 + 8 * odd
        if n == 0:
            return copy(own, dst, DZ, H, H, DY, s_send.at[0], s_recv.at[0], r, sibling)
        if n == 1:
            return copy(own, dst, DZ, 0, 0, H, s_send.at[1], s_recv.at[1], r, sibling)
        if n == 2:
            return copy(own, dst, DZ, H + DY, H + DY, H, s_send.at[2], s_recv.at[2], r, sibling)
        return copy(outer_plane[0], 13 * odd, 1, 0, 0, EY, s_send.at[3], s_recv.at[3], r, sibling)

    for j in range(4):

        @pl.when(has_outer)
        def _(j=j):
            z_copy(j).start()

    @pl.when(has_inner2)
    def _():
        z_copy(4).start()

    def y_start(n):
        up, down = y_copies(n)

        @pl.when(has_up)
        def _():
            up.start()

        @pl.when(has_down)
        def _():
            down.start()

    def y_wait_recv(n):
        up, down = y_copies(n)

        @pl.when(has_down)
        def _():
            up.wait_recv()

        @pl.when(has_up)
        def _():
            down.wait_recv()

    def y_wait_send(n):
        up, down = y_copies(n)

        @pl.when(has_up)
        def _():
            up.wait_send()

        @pl.when(has_down)
        def _():
            down.wait_send()

    y_start(0)
    s_copy(0).start()
    for j in range(H):

        @pl.when(has_outer)
        def _(j=j):
            z_copy(j).wait_recv()
            y_start(j + 1)

    y_wait_recv(0)
    s_copy(1).start()
    s_copy(2).start()

    @pl.when(has_outer)
    def _():
        y_wait_recv(1)

    s_copy(3).start()
    for j in range(1, H):

        @pl.when(has_outer)
        def _(j=j):
            y_wait_recv(j + 1)

    for n in range(4):
        s_copy(n).wait_recv()

    y_first = r * DY - 4
    z_first = c * DZ - 4

    @pl.loop(0, EY - 2)
    def _(q):
        in_y = jnp.logical_and(y_first + q >= 0, y_first + q < rows * DY)

        @pl.loop(0, EZ - 2)
        def _(p):
            inside = jnp.logical_and(in_y, jnp.logical_and(z_first + p >= 0, z_first + p < cols * DZ))
            u = [e[i, p + 1, line(q + 1), :] for i in range(3)]
            grads = [
                [
                    shifted(u[i], 1) - shifted(u[i], -1),
                    e[i, p + 1, line(q + 2), :] - e[i, p + 1, line(q), :],
                    e[i, p + 2, line(q + 1), :] - e[i, p, line(q + 1), :],
                ]
                for i in range(3)
            ]
            strain, quarter = strain_scaled(grads)
            quarter = quarter * jnp.where(inside, 1.0, 0.0)
            for n, (i, j) in enumerate(pair_list):
                t[n, p] = u[i] * u[j]
                t[6 + n, p] = quarter * strain[n]

        @pl.when(jnp.logical_and(q >= 4, q < 4 + DY))
        def _():
            for n in range(6):
                for k in range(DZ):
                    ms[n, k, q - 4] = t[6 + n, k + 4]

        @pl.loop(0, 12)
        def _(n):
            for x in range(0, nt, 8):
                cells = [t[n, p, x : x + 8] for p in range(EZ - 2)]
                for k, value in enumerate(double_box(cells)):
                    zp[n, k, q, x : x + 8] = value

    @pl.loop(0, 3 * EY)
    def _(n):
        i, q = n // EY, lax.rem(n, EY)
        for x in range(0, nt, 8):
            cells = [e[i, p, line(q, x, 8), :] for p in range(EZ)]
            for k, value in enumerate(double_box(cells)):
                zv[i, k, q, x : x + 8] = value

    @pl.loop(0, 12 * DZ)
    def _(n):
        f, k = n // DZ, lax.rem(n, DZ)
        for x in range(0, nt, 8):
            cells = [zp[f, k, q, x : x + 8] for q in range(EY - 2)]
            for y, value in enumerate(double_box(cells)):
                fp[f, k, y, x : x + 8] = value

    @pl.loop(0, 3 * (DZ + 2))
    def _(n):
        i, k = n // (DZ + 2), lax.rem(n, DZ + 2)
        for x in range(0, nt, 8):
            cells = [zv[i, k, q, x : x + 8] for q in range(EY)]
            for y, value in enumerate(double_box(cells)):
                fv[i, k, y, x : x + 8] = value

    for j in range(4):

        @pl.when(has_outer)
        def _(j=j):
            z_copy(j).wait_send()

    @pl.when(has_inner2)
    def _():
        z_copy(4).wait_send()

    y_wait_send(0)
    for j in range(H):

        @pl.when(has_outer)
        def _(j=j):
            y_wait_send(j + 1)

    for n in range(4):
        s_copy(n).wait_send()


def halo(velocity, rows, cols):
    nt = velocity.shape[-1] // 128
    f32 = functools.partial(jax.ShapeDtypeStruct, dtype=jnp.float32)
    in_vmem = pl.BlockSpec(memory_space=VMEM)
    dma = pltpu.SemaphoreType.DMA
    scratch = lambda *shape: pltpu.VMEM((*shape, nt, 128), jnp.float32)
    return pl.pallas_call(
        functools.partial(halo_kernel, rows, cols, nt),
        out_shape=(f32((12, DZ, DY, nt, 128)), f32((3, DZ + 2, DY + 2, nt, 128)), f32((6, DZ, DY, nt, 128))),
        in_specs=[in_vmem],
        out_specs=(in_vmem, in_vmem, in_vmem),
        scratch_shapes=[
            pltpu.VMEM((3, EZ, EY * nt, 128), jnp.float32),
            scratch(12, EZ - 2),
            scratch(12, DZ, EY - 2),
            scratch(3, DZ + 2, EY),
            dma((5,)),
            dma((5,)),
            dma((2, 6)),
            dma((2, 6)),
            dma((4,)),
            dma((4,)),
        ],
        compiler_params=pltpu.CompilerParams(collective_id=0, has_side_effects=True, vmem_limit_bytes=VMEM_LIMIT),
        name="halo",
    )(velocity)


def band_matrix():
    taps = np.array([1, 2, 3, 4, 5, 4, 3, 2, 1], np.float32)
    center = np.zeros((128, 128), np.float32)
    edge = np.zeros((128, 128), np.float32)
    for source in range(128):
        for k in range(9):
            target = source + k - 4
            if 0 <= target < 128:
                center[source, target] = taps[k]
            else:
                edge[source, target % 128] = taps[k]
    half = np.concatenate([center, edge], axis=1)
    return np.concatenate([half, half], axis=0)


def x_filter(values, band):
    rows, nt, _ = values.shape
    flat = values.reshape(rows * nt, 128)
    high = flat.astype(jnp.bfloat16)
    low = (flat - high.astype(jnp.float32)).astype(jnp.bfloat16)
    both = jnp.dot(jnp.concatenate([high, low], axis=1), band, preferred_element_type=jnp.float32)
    center = both[:, :128].reshape(rows, nt, 128)
    edge = both[:, 128:].reshape(rows, nt, 128)
    lane = lax.broadcasted_iota(jnp.int32, (rows, nt, 128), 2)
    beside = jnp.where(lane < 64, pltpu.roll(edge, 1, 1), pltpu.roll(edge, nt - 1, 1))
    return (center + beside) * (1.0 / 15625.0)


def finish_kernel(nt, edges, band, fp, fv, leonard, model, sums, bar, filtered, native):
    k = pl.program_id(0)

    @pl.when(k == 0)
    def _():
        sums[...] = jnp.zeros_like(sums)

        @pl.loop(0, 3 * (DZ + 2))
        def _(n):
            i, plane = n // (DZ + 2), lax.rem(n, DZ + 2)
            keep = jnp.where(plane == 0, edges[0], jnp.where(plane == DZ + 1, edges[1], 1.0))
            bar[i, plane] = x_filter(fv[i, plane], band[...]) * keep
            bar[i, plane, 0] = bar[i, plane, 0] * edges[2]
            bar[i, plane, DY + 1] = bar[i, plane, DY + 1] * edges[3]

    @pl.loop(0, 12)
    def _(n):
        filtered[n] = x_filter(fp[n, 0], band[...])

    @pl.loop(0, DY)
    def _(y):
        u = [bar[i, k + 1, y + 1] for i in range(3)]
        grads = [
            [
                shifted(u[i], 1) - shifted(u[i], -1),
                bar[i, k + 1, y + 2] - bar[i, k + 1, y],
                bar[i, k + 2, y + 1] - bar[i, k, y + 1],
            ]
            for i in range(3)
        ]
        strain, quarter = strain_scaled(grads)
        scaled = 8.0 * quarter
        row = pl.ds(pl.multiple_of(y * nt, 8), nt)
        numer = jnp.zeros((nt, 128), jnp.float32)
        denom = jnp.zeros((nt, 128), jnp.float32)
        for n, (i, j) in enumerate(pair_list):
            leonard_p = filtered[n, y] - u[i] * u[j]
            model_p = 2.0 * filtered[6 + n, y] - scaled * strain[n]
            native[n, row, :] = leonard_p
            native[6 + n, row, :] = model_p
            weighted = pair_weight[n] * model_p
            numer = numer + weighted * leonard_p
            denom = denom + weighted * model_p
        sums[0, pl.ds(y, 1), :] += jnp.sum(numer, axis=0, keepdims=True)
        sums[1, pl.ds(y, 1), :] += jnp.sum(denom, axis=0, keepdims=True)

    @pl.loop(0, 6)
    def _(n):
        for x in range(nt):
            leonard[n, 0, :, x * 128 : (x + 1) * 128] = native[n, pl.ds(x, DY, stride=nt), :]
            model[n, 0, :, x * 128 : (x + 1) * 128] = native[6 + n, pl.ds(x, DY, stride=nt), :]


def finish(fp, fv, edges, width):
    nt = width // 128
    f32 = functools.partial(jax.ShapeDtypeStruct, dtype=jnp.float32)
    scratch = lambda *shape: pltpu.VMEM((*shape, 128), jnp.float32)
    return pl.pallas_call(
        functools.partial(finish_kernel, nt),
        grid=(DZ,),
        out_shape=(f32((6, DZ, DY, width)), f32((6, DZ, DY, width)), f32((2, DY, 128))),
        in_specs=[
            pl.BlockSpec(memory_space=pltpu.MemorySpace.SMEM),
            pl.BlockSpec((256, 256), lambda k: (0, 0)),
            pl.BlockSpec((12, 1, DY, nt, 128), lambda k: (0, k, 0, 0, 0)),
            pl.BlockSpec((3, DZ + 2, DY + 2, nt, 128), lambda k: (0, 0, 0, 0, 0)),
        ],
        out_specs=(
            pl.BlockSpec((6, 1, DY, width), lambda k: (0, k, 0, 0)),
            pl.BlockSpec((6, 1, DY, width), lambda k: (0, k, 0, 0)),
            pl.BlockSpec((2, DY, 128), lambda k: (0, 0, 0)),
        ),
        scratch_shapes=[scratch(3, DZ + 2, DY + 2, nt), scratch(12, DY, nt), scratch(12, DY * nt)],
        compiler_params=pltpu.CompilerParams(vmem_limit_bytes=VMEM_LIMIT),
        name="finish",
    )(edges, jnp.asarray(band_matrix(), jnp.bfloat16), fp, fv)


def total_kernel(cols, points, sums, coeff, parts, send, recv):
    r = lax.axis_index("row")
    c = lax.axis_index("col")
    barrier = pltpu.get_barrier_semaphore()
    for step in range(1, cols):
        pl.semaphore_signal(barrier, inc=1, device_id=(r, lax.rem(c + step, cols)), device_id_type=MESH)
    pl.semaphore_wait(barrier, cols - 1)
    copies = [
        pltpu.make_async_remote_copy(
            src_ref=sums,
            dst_ref=parts.at[step - 1],
            send_sem=send.at[step - 1],
            recv_sem=recv.at[step - 1],
            device_id=(r, lax.rem(c + step, cols)),
            device_id_type=MESH,
        )
        for step in range(1, cols)
    ]
    for one in copies:
        one.start()
    added = sums[...]
    for step, one in enumerate(copies):
        one.wait_recv()
        added = added + parts[step]
    numer = jnp.sum(added[0], axis=1, keepdims=True) / points
    denom = jnp.sum(added[1], axis=1, keepdims=True) / points
    ratio = jnp.maximum(numer / (denom + 1e-06), 0.0)
    coeff[...] = jnp.broadcast_to(-2.0 * ratio, coeff.shape)
    for one in copies:
        one.wait_send()


def total(sums, cols, points):
    in_vmem = pl.BlockSpec(memory_space=VMEM)
    dma = pltpu.SemaphoreType.DMA
    return pl.pallas_call(
        functools.partial(total_kernel, cols, points),
        out_shape=jax.ShapeDtypeStruct((DY, 128), jnp.float32),
        in_specs=[in_vmem],
        out_specs=in_vmem,
        scratch_shapes=[pltpu.VMEM((cols - 1, 2, DY, 128), jnp.float32), dma((cols - 1,)), dma((cols - 1,))],
        compiler_params=pltpu.CompilerParams(collective_id=1, has_side_effects=True),
        name="total",
    )(sums)


def scale_kernel(nt, coeff, ms, stress):
    for k in range(DZ):
        for x in range(nt):
            stress[0, k, :, x * 128 : (x + 1) * 128] = ms[0, k, pl.ds(x, DY, stride=nt), :] * coeff[...]


def scale(coeff, ms, width):
    nt = width // 128
    return pl.pallas_call(
        functools.partial(scale_kernel, nt),
        grid=(6,),
        out_shape=jax.ShapeDtypeStruct((6, DZ, DY, width), jnp.float32),
        in_specs=[
            pl.BlockSpec((DY, 128), lambda n: (0, 0)),
            pl.BlockSpec((1, DZ, DY * nt, 128), lambda n: (n, 0, 0, 0)),
        ],
        out_specs=pl.BlockSpec((1, DZ, DY, width), lambda n: (n, 0, 0, 0)),
        compiler_params=pltpu.CompilerParams(vmem_limit_bytes=VMEM_LIMIT),
        name="scale",
    )(coeff, ms.reshape(6, DZ, DY * nt, 128))


def on_device(velocity):
    rows, cols = lax.axis_size("row"), lax.axis_size("col")
    width = velocity.shape[-1]
    fp, fv, ms = halo(velocity, rows, cols)
    r, c = lax.axis_index("row"), lax.axis_index("col")
    edges = jnp.stack([c > 0, c < cols - 1, r > 0, r < rows - 1]).astype(jnp.float32)
    leonard, model, sums = finish(fp, fv, edges, width)
    coeff = total(sums, cols, width * DZ * cols)
    return leonard, model, scale(coeff, ms, width)


def solution(mesh):
    placed = P(None, "col", "row", None)
    return jax.shard_map(on_device, mesh=mesh, in_specs=(placed,), out_specs=(placed, placed, placed), check_vma=False)
```

```python
import functools

import jax
import jax.numpy as jnp
import numpy as np
from jax import lax
from jax.experimental import pallas as pl
from jax.experimental.pallas import tpu as pltpu
from jax.sharding import PartitionSpec as P

MESH = pl.DeviceIdType.MESH
VMEM = pltpu.MemorySpace.VMEM
pair_list = ((0, 0), (0, 1), (0, 2), (1, 1), (1, 2), (2, 2))
pair_weight = (1.0, 2.0, 2.0, 1.0, 2.0, 1.0)

DZ = 4
DY = 8
H = 5
EZ = DZ + 2 * H
EY = DY + 2 * H
VMEM_LIMIT = 60 * 1024 * 1024


def shifted(u, by):
    nt = u.shape[0]
    lane = lax.broadcasted_iota(jnp.int32, u.shape, 1)
    if by == 1:
        near = pltpu.roll(u, 127, 1)
        return jnp.where(lane == 127, pltpu.roll(near, nt - 1, 0), near)
    near = pltpu.roll(u, 1, 1)
    return jnp.where(lane == 0, pltpu.roll(near, 1, 0), near)


def double_box(cells):
    for _ in range(2):
        two = [a + b for a, b in zip(cells, cells[1:])]
        four = [a + b for a, b in zip(two, two[2:])]
        cells = [a + b for a, b in zip(four, cells[4:])]
    return cells


def strain_scaled(grads):
    diag = [grads[i][i] for i in range(3)]
    off = [grads[i][j] + grads[j][i] for i, j in ((0, 1), (0, 2), (1, 2))]
    total = 2.0 * (diag[0] * diag[0] + diag[1] * diag[1] + diag[2] * diag[2])
    total = total + (off[0] * off[0] + off[1] * off[1] + off[2] * off[2])
    quarter = jnp.sqrt(total * (1.0 / 64.0))
    diag = [d + d for d in diag]
    return (diag[0], off[0], off[1], diag[1], off[2], diag[2]), quarter


def halo_kernel(rows, cols, nt, vel, fp_out, fv_out, ms_out, e, t, zp, zv, fp, fv, ms, z_send, z_recv, y_send, y_recv, s_send, s_recv, o_sem):
    groups = nt // 8
    cuts = [7] + [17 + 8 * g for g in range(groups - 1)] + [7 + nt]
    r = lax.axis_index("row")
    c = lax.axis_index("col")
    odd = lax.rem(c, 2)
    out = 2 * odd - 1
    sibling = c - out
    outer1, outer2, inner2 = c + out, c + 2 * out, c - 2 * out
    has_outer = jnp.logical_and(outer1 >= 0, outer1 < cols)
    has_inner2 = jnp.logical_and(inner2 >= 0, inner2 < cols)
    has_up = r > 0
    has_down = r < rows - 1

    barrier = pltpu.get_barrier_semaphore()
    partners = (
        (has_up, r - 1, c),
        (has_down, r + 1, c),
        (c >= 0, r, sibling),
        (has_outer, r, outer1),
        (has_outer, r, outer2),
        (has_inner2, r, inner2),
    )
    count = 0
    for there, row, col in partners:

        @pl.when(there)
        def _(row=row, col=col):
            pl.semaphore_signal(barrier, inc=1, device_id=(row, col), device_id_type=MESH)

        count = count + there.astype(jnp.int32)

    @pl.loop(0, 3 * DZ)
    def _(n):
        i, k = n // DZ, lax.rem(n, DZ)
        for x in range(0, nt, 8):
            e[i, H + k, H : H + DY, 8 + x : 16 + x, :] = vel[i, k, :, x * 128 : (x + 8) * 128].reshape(DY, 8, 128)
        e[i, H + k, H : H + DY, 7:8, :] = vel[i, k, :, (nt - 1) * 128 :].reshape(DY, 1, 128)

    zero = jnp.zeros((nt + 16, 128), jnp.float32)
    mine = H * odd

    def clear(plane0, planes, row0, count_rows):
        @pl.loop(0, 3 * planes * count_rows)
        def _(n):
            i, rest = n // (planes * count_rows), lax.rem(n, planes * count_rows)
            e[i, plane0 + rest // count_rows, row0 + lax.rem(rest, count_rows)] = zero

    @pl.when(jnp.logical_not(has_up))
    def _():
        clear(mine, EZ - H, 0, H)

    @pl.when(jnp.logical_not(has_down))
    def _():
        clear(mine, EZ - H, H + DY, H)

    @pl.when(jnp.logical_not(has_outer))
    def _():
        clear(odd * (H + DZ), H, 0, EY)

    pl.semaphore_wait(barrier, count)

    def copy(g, p_src, p_dst, planes, q_src, q_dst, count_rows, send, recv, row, col):
        tiles = pl.ds(cuts[g], cuts[g + 1] - cuts[g])
        return pltpu.make_async_remote_copy(
            src_ref=e.at[:, pl.ds(p_src, planes), pl.ds(q_src, count_rows), tiles],
            dst_ref=e.at[:, pl.ds(p_dst, planes), pl.ds(q_dst, count_rows), tiles],
            send_sem=send,
            recv_sem=recv,
            device_id=(row, col),
            device_id_type=MESH,
        )

    own = H
    far = odd * (H + DZ)
    near = 4 + 5 * odd

    def z_copies(g):
        return (
            (has_outer, copy(g, own, 9 - 8 * odd, DZ, H, H, DY, z_send.at[g, 0], z_recv.at[g, 0], r, outer1), has_outer),
            (has_inner2, copy(g, 8 - 3 * odd, 13 * odd, 1, H, H, DY, z_send.at[g, 1], z_recv.at[g, 1], r, inner2), has_outer),
        )

    def y_copies(g, kind):
        plane, planes = ((own, DZ), (far, H))[kind]
        on = jnp.logical_or(kind == 0, has_outer)
        up_there, down_there = jnp.logical_and(has_up, on), jnp.logical_and(has_down, on)
        up = copy(g, plane, plane, planes, H, H + DY, H, y_send.at[g, 0, kind], y_recv.at[g, 0, kind], r - 1, c)
        down = copy(g, plane, plane, planes, DY, 0, H, y_send.at[g, 1, kind], y_recv.at[g, 1, kind], r + 1, c)
        return (up_there, up, down_there), (down_there, down, up_there)

    def s_copies(g):
        dst = 1 + 8 * odd
        yes = c >= 0
        plan = ((own, dst, DZ, H, DY), (own, dst, DZ, 0, H), (own, dst, DZ, H + DY, H), (near, 13 * odd, 1, 0, EY))
        return [
            (yes, copy(g, src, to, planes, q, q, n, s_send.at[g, m], s_recv.at[g, m], r, sibling), yes)
            for m, (src, to, planes, q, n) in enumerate(plan)
        ]

    def start(copies):
        for sends, one, _ in copies:
            pl.when(sends)(one.start)

    def wait_recv(copies):
        for _, one, receives in copies:
            pl.when(receives)(one.wait_recv)

    def wait_send(copies):
        for sends, one, _ in copies:
            pl.when(sends)(one.wait_send)

    def forward(g):
        wait_recv(z_copies(g))
        start(y_copies(g, 1))

    def share(g):
        wait_recv(y_copies(g, 0))
        wait_recv(y_copies(g, 1))
        start(s_copies(g)[1:])

    for g in range(groups):
        start(z_copies(g))
        start(y_copies(g, 0))
        start(s_copies(g)[:1])

    for g in range(min(2, groups)):
        forward(g)
    share(0)

    y_first = r * DY - 4
    z_first = c * DZ - 4

    def results(x):
        tiles = pl.ds(x, 8)
        g = x // 8
        return (
            pltpu.make_async_copy(fp.at[:, :, :, tiles], fp_out.at[:, :, :, tiles], o_sem.at[g, 0]),
            pltpu.make_async_copy(fv.at[:, :, :, tiles], fv_out.at[:, :, :, tiles], o_sem.at[g, 1]),
            pltpu.make_async_copy(ms.at[:, :, pl.ds(4, DY), tiles], ms_out.at[:, :, :, tiles], o_sem.at[g, 2]),
        )

    lane = lax.broadcasted_iota(jnp.int32, (8, 128), 1)

    def compute(x):
        at = pl.ds(pl.multiple_of(8 + x, 8), 8)
        before, after = pl.ds(7 + x, 8), pl.ds(9 + x, 8)
        to = pl.ds(pl.multiple_of(x, 8), 8)

        @pl.loop(0, EY - 2)
        def _(q):
            in_y = jnp.where(jnp.logical_and(y_first + q >= 0, y_first + q < rows * DY), 1.0, 0.0)
            for p in range(EZ - 2):
                grads = []
                for i in range(3):
                    u = e[i, p + 1, q + 1, at, :]
                    right = pltpu.roll(jnp.where(lane == 0, e[i, p + 1, q + 1, after, :], u), 127, 1)
                    left = pltpu.roll(jnp.where(lane == 127, e[i, p + 1, q + 1, before, :], u), 1, 1)
                    grads.append(
                        [
                            right - left,
                            e[i, p + 1, q + 2, at, :] - e[i, p + 1, q, at, :],
                            e[i, p + 2, q + 1, at, :] - e[i, p, q + 1, at, :],
                        ]
                    )
                strain, quarter = strain_scaled(grads)
                in_z = jnp.logical_and(z_first + p >= 0, z_first + p < cols * DZ)
                quarter = quarter * jnp.where(in_z, in_y, 0.0)
                for n in range(6):
                    value = quarter * strain[n]
                    t[n, p] = value
                    if 4 <= p < 4 + DZ:
                        ms[n, p - 4, q, to, :] = value
            for n, (i, j) in enumerate(pair_list):
                cells = [e[i, p, q + 1, at, :] * e[j, p, q + 1, at, :] for p in range(1, EZ - 1)]
                for k, value in enumerate(double_box(cells)):
                    zp[n, k, q] = value
                for k, value in enumerate(double_box([t[n, p] for p in range(EZ - 2)])):
                    zp[6 + n, k, q] = value

        @pl.loop(0, EY)
        def _(q):
            for i in range(3):
                for k, value in enumerate(double_box([e[i, p, q, at, :] for p in range(EZ)])):
                    zv[i, k, q] = value

        @pl.loop(0, 12)
        def _(f):
            for k in range(DZ):
                for y, value in enumerate(double_box([zp[f, k, q] for q in range(EY - 2)])):
                    fp[f, k, y, to, :] = value

        @pl.loop(0, DZ + 2)
        def _(k):
            for i in range(3):
                for y, value in enumerate(double_box([zv[i, k, q] for q in range(EY)])):
                    fv[i, k, y, to, :] = value

        for one in results(x):
            one.start()

    @pl.loop(0, groups)
    def _(g):
        for step in range(groups):

            @pl.when(g == step)
            def _(step=step):
                wait_recv(s_copies(step))
                if step == groups - 1:

                    @pl.loop(0, 3 * EZ)
                    def _(n):
                        i, p = n // EZ, lax.rem(n, EZ)
                        e[i, p, :, 7 + nt : 9 + nt, :] = e[i, p, :, 7:9, :]

        compute(g * 8)
        for step in range(groups):

            @pl.when(g == step)
            def _(step=step):
                if step + 2 < groups:
                    forward(step + 2)
                if step + 1 < groups:
                    share(step + 1)

    for g in range(groups):
        for one in results(8 * g):
            one.wait()
        wait_send(z_copies(g))
        wait_send(y_copies(g, 0))
        wait_send(y_copies(g, 1))
        wait_send(s_copies(g))


def halo(velocity, rows, cols):
    nt = velocity.shape[-1] // 128
    groups = nt // 8
    f32 = functools.partial(jax.ShapeDtypeStruct, dtype=jnp.float32)
    in_hbm = pl.BlockSpec(memory_space=pl.ANY)
    dma = pltpu.SemaphoreType.DMA
    scratch = lambda *shape: pltpu.VMEM((*shape, 128), jnp.float32)
    return pl.pallas_call(
        functools.partial(halo_kernel, rows, cols, nt),
        out_shape=(f32((12, DZ, DY, nt, 128)), f32((3, DZ + 2, DY + 2, nt, 128)), f32((6, DZ, DY, nt, 128))),
        in_specs=[pl.BlockSpec(memory_space=VMEM)],
        out_specs=(in_hbm, in_hbm, in_hbm),
        scratch_shapes=[
            scratch(3, EZ, EY, nt + 16),
            scratch(6, EZ - 2, 8),
            scratch(12, DZ, EY - 2, 8),
            scratch(3, DZ + 2, EY, 8),
            scratch(12, DZ, DY, nt),
            scratch(3, DZ + 2, DY + 2, nt),
            scratch(6, DZ, EY - 2, nt),
            dma((groups, 2)),
            dma((groups, 2)),
            dma((groups, 2, 2)),
            dma((groups, 2, 2)),
            dma((groups, 4)),
            dma((groups, 4)),
            dma((groups, 3)),
        ],
        compiler_params=pltpu.CompilerParams(collective_id=0, has_side_effects=True, vmem_limit_bytes=VMEM_LIMIT),
        name="halo",
    )(velocity)


def band_matrix():
    taps = np.array([1, 2, 3, 4, 5, 4, 3, 2, 1], np.float32)
    center = np.zeros((128, 128), np.float32)
    edge = np.zeros((128, 128), np.float32)
    for source in range(128):
        for k in range(9):
            target = source + k - 4
            if 0 <= target < 128:
                center[source, target] = taps[k]
            else:
                edge[source, target % 128] = taps[k]
    half = np.concatenate([center, edge], axis=1)
    return np.concatenate([half, half], axis=0)


def x_filter(values, band):
    rows, nt, _ = values.shape
    flat = values.reshape(rows * nt, 128)
    high = flat.astype(jnp.bfloat16)
    low = (flat - high.astype(jnp.float32)).astype(jnp.bfloat16)
    both = jnp.dot(jnp.concatenate([high, low], axis=1), band, preferred_element_type=jnp.float32)
    center = both[:, :128].reshape(rows, nt, 128)
    edge = both[:, 128:].reshape(rows, nt, 128)
    lane = lax.broadcasted_iota(jnp.int32, (rows, nt, 128), 2)
    beside = jnp.where(lane < 64, pltpu.roll(edge, 1, 1), pltpu.roll(edge, nt - 1, 1))
    return (center + beside) * (1.0 / 15625.0)


def finish_kernel(nt, edges, band, fp, fv, leonard, model, sums, bar, filtered, native):
    k = pl.program_id(0)

    @pl.when(k == 0)
    def _():
        sums[...] = jnp.zeros_like(sums)

        @pl.loop(0, 3 * (DZ + 2))
        def _(n):
            i, plane = n // (DZ + 2), lax.rem(n, DZ + 2)
            keep = jnp.where(plane == 0, edges[0], jnp.where(plane == DZ + 1, edges[1], 1.0))
            bar[i, plane] = x_filter(fv[i, plane], band[...]) * keep
            bar[i, plane, 0] = bar[i, plane, 0] * edges[2]
            bar[i, plane, DY + 1] = bar[i, plane, DY + 1] * edges[3]

    @pl.loop(0, 12)
    def _(n):
        filtered[n] = x_filter(fp[n, 0], band[...])

    @pl.loop(0, DY)
    def _(y):
        u = [bar[i, k + 1, y + 1] for i in range(3)]
        grads = [
            [
                shifted(u[i], 1) - shifted(u[i], -1),
                bar[i, k + 1, y + 2] - bar[i, k + 1, y],
                bar[i, k + 2, y + 1] - bar[i, k, y + 1],
            ]
            for i in range(3)
        ]
        strain, quarter = strain_scaled(grads)
        scaled = 8.0 * quarter
        row = pl.ds(pl.multiple_of(y * nt, 8), nt)
        numer = jnp.zeros((nt, 128), jnp.float32)
        denom = jnp.zeros((nt, 128), jnp.float32)
        for n, (i, j) in enumerate(pair_list):
            leonard_p = filtered[n, y] - u[i] * u[j]
            model_p = 2.0 * filtered[6 + n, y] - scaled * strain[n]
            native[n, row, :] = leonard_p
            native[6 + n, row, :] = model_p
            weighted = pair_weight[n] * model_p
            numer = numer + weighted * leonard_p
            denom = denom + weighted * model_p
        sums[0, pl.ds(y, 1), :] += jnp.sum(numer, axis=0, keepdims=True)
        sums[1, pl.ds(y, 1), :] += jnp.sum(denom, axis=0, keepdims=True)

    @pl.loop(0, 6)
    def _(n):
        for x in range(nt):
            leonard[n, 0, :, x * 128 : (x + 1) * 128] = native[n, pl.ds(x, DY, stride=nt), :]
            model[n, 0, :, x * 128 : (x + 1) * 128] = native[6 + n, pl.ds(x, DY, stride=nt), :]


def finish(fp, fv, edges, width):
    nt = width // 128
    f32 = functools.partial(jax.ShapeDtypeStruct, dtype=jnp.float32)
    scratch = lambda *shape: pltpu.VMEM((*shape, 128), jnp.float32)
    return pl.pallas_call(
        functools.partial(finish_kernel, nt),
        grid=(DZ,),
        out_shape=(f32((6, DZ, DY, width)), f32((6, DZ, DY, width)), f32((2, DY, 128))),
        in_specs=[
            pl.BlockSpec(memory_space=pltpu.MemorySpace.SMEM),
            pl.BlockSpec((256, 256), lambda k: (0, 0)),
            pl.BlockSpec((12, 1, DY, nt, 128), lambda k: (0, k, 0, 0, 0)),
            pl.BlockSpec((3, DZ + 2, DY + 2, nt, 128), lambda k: (0, 0, 0, 0, 0)),
        ],
        out_specs=(
            pl.BlockSpec((6, 1, DY, width), lambda k: (0, k, 0, 0)),
            pl.BlockSpec((6, 1, DY, width), lambda k: (0, k, 0, 0)),
            pl.BlockSpec((2, DY, 128), lambda k: (0, 0, 0)),
        ),
        scratch_shapes=[scratch(3, DZ + 2, DY + 2, nt), scratch(12, DY, nt), scratch(12, DY * nt)],
        compiler_params=pltpu.CompilerParams(vmem_limit_bytes=VMEM_LIMIT),
        name="finish",
    )(edges, jnp.asarray(band_matrix(), jnp.bfloat16), fp, fv)


def total_kernel(cols, points, sums, coeff, parts, send, recv):
    r = lax.axis_index("row")
    c = lax.axis_index("col")
    barrier = pltpu.get_barrier_semaphore()
    for step in range(1, cols):
        pl.semaphore_signal(barrier, inc=1, device_id=(r, lax.rem(c + step, cols)), device_id_type=MESH)
    pl.semaphore_wait(barrier, cols - 1)
    copies = [
        pltpu.make_async_remote_copy(
            src_ref=sums,
            dst_ref=parts.at[step - 1],
            send_sem=send.at[step - 1],
            recv_sem=recv.at[step - 1],
            device_id=(r, lax.rem(c + step, cols)),
            device_id_type=MESH,
        )
        for step in range(1, cols)
    ]
    for one in copies:
        one.start()
    added = sums[...]
    for step, one in enumerate(copies):
        one.wait_recv()
        added = added + parts[step]
    numer = jnp.sum(added[0], axis=1, keepdims=True) / points
    denom = jnp.sum(added[1], axis=1, keepdims=True) / points
    ratio = jnp.maximum(numer / (denom + 1e-06), 0.0)
    coeff[...] = jnp.broadcast_to(-2.0 * ratio, coeff.shape)
    for one in copies:
        one.wait_send()


def total(sums, cols, points):
    in_vmem = pl.BlockSpec(memory_space=VMEM)
    dma = pltpu.SemaphoreType.DMA
    return pl.pallas_call(
        functools.partial(total_kernel, cols, points),
        out_shape=jax.ShapeDtypeStruct((DY, 128), jnp.float32),
        in_specs=[in_vmem],
        out_specs=in_vmem,
        scratch_shapes=[pltpu.VMEM((cols - 1, 2, DY, 128), jnp.float32), dma((cols - 1,)), dma((cols - 1,))],
        compiler_params=pltpu.CompilerParams(collective_id=1, has_side_effects=True),
        name="total",
    )(sums)


def scale_kernel(nt, coeff, ms, stress):
    for k in range(DZ):
        for x in range(nt):
            stress[0, k, :, x * 128 : (x + 1) * 128] = ms[0, k, pl.ds(x, DY, stride=nt), :] * coeff[...]


def scale(coeff, ms, width):
    nt = width // 128
    return pl.pallas_call(
        functools.partial(scale_kernel, nt),
        grid=(6,),
        out_shape=jax.ShapeDtypeStruct((6, DZ, DY, width), jnp.float32),
        in_specs=[
            pl.BlockSpec((DY, 128), lambda n: (0, 0)),
            pl.BlockSpec((1, DZ, DY * nt, 128), lambda n: (n, 0, 0, 0)),
        ],
        out_specs=pl.BlockSpec((1, DZ, DY, width), lambda n: (n, 0, 0, 0)),
        compiler_params=pltpu.CompilerParams(vmem_limit_bytes=VMEM_LIMIT),
        name="scale",
    )(coeff, ms.reshape(6, DZ, DY * nt, 128))


def on_device(velocity):
    rows, cols = lax.axis_size("row"), lax.axis_size("col")
    width = velocity.shape[-1]
    fp, fv, ms = halo(velocity, rows, cols)
    r, c = lax.axis_index("row"), lax.axis_index("col")
    edges = jnp.stack([c > 0, c < cols - 1, r > 0, r < rows - 1]).astype(jnp.float32)
    leonard, model, sums = finish(fp, fv, edges, width)
    coeff = total(sums, cols, width * DZ * cols)
    return leonard, model, scale(coeff, ms, width)


def solution(mesh):
    placed = P(None, "col", "row", None)
    return jax.shard_map(on_device, mesh=mesh, in_specs=(placed,), out_specs=(placed, placed, placed), check_vma=False)
```

```python
import functools

import jax
import jax.numpy as jnp
import numpy as np
from jax import lax
from jax.experimental import pallas as pl
from jax.experimental.pallas import tpu as pltpu
from jax.sharding import PartitionSpec as P

MESH = pl.DeviceIdType.MESH
VMEM = pltpu.MemorySpace.VMEM
pair_list = ((0, 0), (0, 1), (0, 2), (1, 1), (1, 2), (2, 2))
pair_weight = (1.0, 2.0, 2.0, 1.0, 2.0, 1.0)

DZ = 4
DY = 8
H = 5
EZ = DZ + 2 * H
EY = DY + 2 * H
VMEM_LIMIT = 60 * 1024 * 1024
FIRST = (("y0", "z0", "s0", "y1", "s1", "y2", "s2", "y3", "s3"), ("p0", "z1", "p1", "z2", "p2", "z3", "p3", "f0"))
LATER = (("f1", "h0"), ("f2", "h1"), ("f3", "h2"), ("h3",))


def shifted(u, by):
    nt = u.shape[0]
    lane = lax.broadcasted_iota(jnp.int32, u.shape, 1)
    if by == 1:
        near = pltpu.roll(u, 127, 1)
        return jnp.where(lane == 127, pltpu.roll(near, nt - 1, 0), near)
    near = pltpu.roll(u, 1, 1)
    return jnp.where(lane == 0, pltpu.roll(near, 1, 0), near)


def double_box(cells):
    for _ in range(2):
        two = [a + b for a, b in zip(cells, cells[1:])]
        four = [a + b for a, b in zip(two, two[2:])]
        cells = [a + b for a, b in zip(four, cells[4:])]
    return cells


def strain_scaled(grads):
    diag = [grads[i][i] for i in range(3)]
    off = [grads[i][j] + grads[j][i] for i, j in ((0, 1), (0, 2), (1, 2))]
    total = 2.0 * (diag[0] * diag[0] + diag[1] * diag[1] + diag[2] * diag[2])
    total = total + (off[0] * off[0] + off[1] * off[1] + off[2] * off[2])
    quarter = jnp.sqrt(total * (1.0 / 64.0))
    diag = [d + d for d in diag]
    return (diag[0], off[0], off[1], diag[1], off[2], diag[2]), quarter


def halo_kernel(rows, cols, nt, vel, fp_out, fv_out, ms_out, e, t, msr, turn, zp, zv, fp, fv, ms, z_send, z_recv, y_send, y_recv, s_send, s_recv, o_sem):
    groups = nt // 8
    cuts = [7] + [17 + 8 * g for g in range(groups - 1)] + [7 + nt]
    r = lax.axis_index("row")
    c = lax.axis_index("col")
    odd = lax.rem(c, 2)
    out = 2 * odd - 1
    sibling = c - out
    outer1, outer2, inner2 = c + out, c + 2 * out, c - 2 * out
    has_outer = jnp.logical_and(outer1 >= 0, outer1 < cols)
    has_inner2 = jnp.logical_and(inner2 >= 0, inner2 < cols)
    place = lax.rem(r, 4)
    helps = jnp.logical_and(jnp.logical_or(place == 1, place == 2), has_outer)
    helped = jnp.logical_and(jnp.logical_or(place == 0, place == 3), has_outer)
    mate = r + 1 - 2 * lax.rem(r, 2)
    has_up = r > 0
    has_down = r < rows - 1

    barrier = pltpu.get_barrier_semaphore()
    partners = (
        (has_up, r - 1, c),
        (has_down, r + 1, c),
        (c >= 0, r, sibling),
        (has_outer, r, outer1),
        (has_outer, r, outer2),
        (has_inner2, r, inner2),
        (has_outer, mate, outer1),
    )
    count = 0
    for there, row, col in partners:

        @pl.when(there)
        def _(row=row, col=col):
            pl.semaphore_signal(barrier, inc=1, device_id=(row, col), device_id_type=MESH)

        count = count + there.astype(jnp.int32)

    @pl.loop(0, 3 * DZ)
    def _(n):
        i, k = n // DZ, lax.rem(n, DZ)
        for x in range(0, nt, 8):
            e[i, H + k, H : H + DY, 8 + x : 16 + x, :] = vel[i, k, :, x * 128 : (x + 8) * 128].reshape(DY, 8, 128)
        e[i, H + k, H : H + DY, 7:8, :] = vel[i, k, :, (nt - 1) * 128 :].reshape(DY, 1, 128)

    zero = jnp.zeros((nt + 16, 128), jnp.float32)
    mine = H * odd

    def clear(plane0, planes, row0, count_rows):
        @pl.loop(0, 3 * planes * count_rows)
        def _(n):
            i, rest = n // (planes * count_rows), lax.rem(n, planes * count_rows)
            e[i, plane0 + rest // count_rows, row0 + lax.rem(rest, count_rows)] = zero

    @pl.when(jnp.logical_not(has_up))
    def _():
        clear(mine, EZ - H, 0, H)

    @pl.when(jnp.logical_not(has_down))
    def _():
        clear(mine, EZ - H, H + DY, H)

    @pl.when(jnp.logical_not(has_outer))
    def _():
        clear(odd * (H + DZ), H, 0, EY)

    pl.semaphore_wait(barrier, count)

    def copy(g, p_src, p_dst, planes, q_src, q_dst, count_rows, send, recv, row, col):
        tiles = pl.ds(cuts[g], cuts[g + 1] - cuts[g])
        return pltpu.make_async_remote_copy(
            src_ref=e.at[:, pl.ds(p_src, planes), pl.ds(q_src, count_rows), tiles],
            dst_ref=e.at[:, pl.ds(p_dst, planes), pl.ds(q_dst, count_rows), tiles],
            send_sem=send,
            recv_sem=recv,
            device_id=(row, col),
            device_id_type=MESH,
        )

    own = H
    far = odd * (H + DZ)
    near = 4 + 5 * odd

    def z_copies(g):
        single = copy(g, 8 - 3 * odd, 13 * odd, 1, H, H, DY, z_send.at[g, 0], z_recv.at[g, 0], r, inner2)
        whole = copy(g, own, 9 - 8 * odd, DZ, H, H, DY, z_send.at[g, 1], z_recv.at[g, 1], r, outer1)
        row = jnp.where(place == 0, H, H + 5)
        part = copy(g, own, 9 - 8 * odd, DZ, row, row, DY - H, z_send.at[g, 2], z_recv.at[g, 2], r, outer1)
        return (helped, part, helped), (helps, whole, helps), (has_inner2, single, has_outer)

    def proxy_copies(g):
        low = place < 2
        src, dst = jnp.where(low, 0, H + DY), jnp.where(low, DY, H)
        one = copy(g, own, 9 - 8 * odd, DZ, src, dst, H, z_send.at[g, 3], z_recv.at[g, 3], mate, outer1)
        return ((helps, one, helped),)

    def y_copies(g, kind):
        plane, planes = ((own, DZ), (far, H))[kind]
        on = jnp.logical_or(kind == 0, has_outer)
        up_there, down_there = jnp.logical_and(has_up, on), jnp.logical_and(has_down, on)
        up = copy(g, plane, plane, planes, H, H + DY, H, y_send.at[g, 0, kind], y_recv.at[g, 0, kind], r - 1, c)
        down = copy(g, plane, plane, planes, DY, 0, H, y_send.at[g, 1, kind], y_recv.at[g, 1, kind], r + 1, c)
        return (up_there, up, down_there), (down_there, down, up_there)

    def s_copies(g):
        dst = 1 + 8 * odd
        yes = c >= 0
        plan = ((own, dst, DZ, H, DY), (own, dst, DZ, 0, H), (own, dst, DZ, H + DY, H))
        plan = plan + tuple((near, 13 * odd, 1, q, n) for _, _, _, q, n in plan)
        return [
            (yes, copy(g, src, to, planes, q, q, n, s_send.at[g, m], s_recv.at[g, m], r, sibling), yes)
            for m, (src, to, planes, q, n) in enumerate(plan)
        ]

    def start(copies):
        for sends, one, _ in copies:
            pl.when(sends)(one.start)

    def wait_recv(copies):
        for _, one, receives in copies:
            pl.when(receives)(one.wait_recv)

    def wait_send(copies):
        for sends, one, _ in copies:
            pl.when(sends)(one.wait_send)

    def proxy(g):
        wait_recv(y_copies(g, 0))
        start(proxy_copies(g))
        start(s_copies(g)[1:3])

    def forward(g):
        wait_recv(z_copies(g))
        wait_recv(proxy_copies(g))
        start(y_copies(g, 1))
        start(s_copies(g)[3:4])

    def share(g):
        wait_recv(y_copies(g, 1))
        start(s_copies(g)[4:])

    acts = {
        "z": lambda g: start(z_copies(g)),
        "y": lambda g: start(y_copies(g, 0)),
        "s": lambda g: start(s_copies(g)[:1]),
        "p": proxy,
        "f": forward,
        "h": share,
    }

    def run(plan):
        for act in plan:
            if int(act[1]) < groups:
                acts[act[0]](int(act[1]))

    for plan in FIRST:
        run(plan)

    y_first = r * DY - 4
    z_first = c * DZ - 4

    def results(x):
        tiles = pl.ds(x * DY if isinstance(x, int) else pl.multiple_of(x * DY, 64), 8 * DY)
        lanes = pl.ds(x * 128 if isinstance(x, int) else pl.multiple_of(x * 128, 1024), 1024)
        g = x // 8
        return (
            pltpu.make_async_copy(fp.at[:, :, tiles], fp_out.at[:, :, tiles], o_sem.at[g, 0]),
            pltpu.make_async_copy(fv.at[:, :, :, tiles], fv_out.at[:, :, :, tiles], o_sem.at[g, 1]),
            pltpu.make_async_copy(ms.at[:, :, :, lanes], ms_out.at[:, :, :, lanes], o_sem.at[g, 2]),
        )

    lane = lax.broadcasted_iota(jnp.int32, (8, 128), 1)

    def compute(x, rest):
        at = pl.ds(pl.multiple_of(8 + x, 8), 8)
        before, after = pl.ds(7 + x, 8), pl.ds(9 + x, 8)
        to = pl.ds(pl.multiple_of(x, 8), 8)

        @pl.loop(6 * rest, 6 + 10 * rest)
        def _(m):
            q = jnp.where(m < 6, m + 5, jnp.where(m < 11, m - 6, m))
            in_y = jnp.where(jnp.logical_and(y_first + q >= 0, y_first + q < rows * DY), 1.0, 0.0)
            for p in range(EZ - 2):
                grads = []
                for i in range(3):
                    u = e[i, p + 1, q + 1, at, :]
                    right = pltpu.roll(jnp.where(lane == 0, e[i, p + 1, q + 1, after, :], u), 127, 1)
                    left = pltpu.roll(jnp.where(lane == 127, e[i, p + 1, q + 1, before, :], u), 1, 1)
                    grads.append(
                        [
                            right - left,
                            e[i, p + 1, q + 2, at, :] - e[i, p + 1, q, at, :],
                            e[i, p + 2, q + 1, at, :] - e[i, p, q + 1, at, :],
                        ]
                    )
                strain, quarter = strain_scaled(grads)
                in_z = jnp.logical_and(z_first + p >= 0, z_first + p < cols * DZ)
                quarter = quarter * jnp.where(in_z, in_y, 0.0)
                for n in range(6):
                    value = quarter * strain[n]
                    t[n, p] = value
                    if 4 <= p < 4 + DZ:
                        msr[n, p - 4, pl.ds(pl.multiple_of(q * 8, 8), 8), :] = value
            for n, (i, j) in enumerate(pair_list):
                cells = [e[i, p, q + 1, at, :] * e[j, p, q + 1, at, :] for p in range(1, EZ - 1)]
                for k, value in enumerate(double_box(cells)):
                    zp[n, k, q] = value
                for k, value in enumerate(double_box([t[n, p] for p in range(EZ - 2)])):
                    zp[6 + n, k, q] = value

        @pl.loop(DY * rest, DY + 2 * H * rest)
        def _(m):
            q = jnp.where(m < DY, m + H, jnp.where(m < DY + H, m - DY, m))
            for i in range(3):
                for k, value in enumerate(double_box([e[i, p, q, at, :] for p in range(EZ)])):
                    zv[i, k, q] = value

        @pl.when(rest == 1)
        def _():
            @pl.loop(0, 6)
            def _(n):
                for k in range(DZ):
                    for j in range(8):
                        ms[n, k, :, pl.ds(pl.multiple_of((x + j) * 128, 128), 128)] = msr[n, k, pl.ds(4 * 8 + j, DY, stride=8), :]

            def turned(slot, dst, values):
                for y, value in enumerate(values):
                    turn[slot, y * 8 : (y + 1) * 8, :] = value
                for j in range(8):
                    dst[pl.ds(pl.multiple_of((x + j) * DY, DY), DY), :] = turn[slot, pl.ds(j, DY, stride=8), :]

            @pl.loop(0, 12)
            def _(f):
                for k in range(DZ):
                    turned(k, fp.at[f, k], double_box([zp[f, k, q] for q in range(EY - 2)]))

            @pl.loop(0, DZ + 2)
            def _(k):
                for i in range(3):
                    values = double_box([zv[i, k, q] for q in range(EY)])
                    turned(2 * i, fv.at[i, k, 0], values[1 : DY + 1])
                    turned(2 * i + 1, fv.at[i, k, 1], [values[DY + 1]] + [values[0]] * (DY - 1))

            for one in results(x):
                one.start()

    @pl.loop(0, 2 * groups)
    def _(turn_of):
        g, rest = turn_of // 2, lax.rem(turn_of, 2)
        for step in range(groups):

            @pl.when(turn_of == 2 * step)
            def _(step=step):
                wait_recv(s_copies(step)[0:4:3])
                if step == groups - 1:

                    @pl.loop(0, 3 * EZ)
                    def _(n):
                        i, p = n // EZ, lax.rem(n, EZ)
                        e[i, p, :, 7 + nt : 9 + nt, :] = e[i, p, :, 7:9, :]

            @pl.when(turn_of == 2 * step + 1)
            def _(step=step):
                wait_recv(s_copies(step)[1:3])
                wait_recv(s_copies(step)[4:])

        compute(g * 8, rest)
        for step in range(groups):

            @pl.when(turn_of == 2 * step)
            def _(step=step):
                run(LATER[step])

    for g in range(groups):
        for one in results(8 * g):
            one.wait()
        wait_send(z_copies(g))
        wait_send(proxy_copies(g))
        wait_send(y_copies(g, 0))
        wait_send(y_copies(g, 1))
        wait_send(s_copies(g))


def halo(velocity, rows, cols):
    nt = velocity.shape[-1] // 128
    groups = nt // 8
    f32 = functools.partial(jax.ShapeDtypeStruct, dtype=jnp.float32)
    in_hbm = pl.BlockSpec(memory_space=pl.ANY)
    dma = pltpu.SemaphoreType.DMA
    scratch = lambda *shape: pltpu.VMEM((*shape, 128), jnp.float32)
    return pl.pallas_call(
        functools.partial(halo_kernel, rows, cols, nt),
        out_shape=(f32((12, DZ, nt * DY, 128)), f32((3, DZ + 2, 2, nt * DY, 128)), f32((6, DZ, DY, nt * 128))),
        in_specs=[pl.BlockSpec(memory_space=VMEM)],
        out_specs=(in_hbm, in_hbm, in_hbm),
        scratch_shapes=[
            scratch(3, EZ, EY, nt + 16),
            scratch(6, EZ - 2, 8),
            scratch(6, DZ, (EY - 2) * 8),
            scratch(6, 8 * DY),
            scratch(12, DZ, EY - 2, 8),
            scratch(3, DZ + 2, EY, 8),
            scratch(12, DZ, nt * DY),
            scratch(3, DZ + 2, 2, nt * DY),
            pltpu.VMEM((6, DZ, DY, nt * 128), jnp.float32),
            dma((groups, 4)),
            dma((groups, 4)),
            dma((groups, 2, 2)),
            dma((groups, 2, 2)),
            dma((groups, 6)),
            dma((groups, 6)),
            dma((groups, 3)),
        ],
        compiler_params=pltpu.CompilerParams(collective_id=0, has_side_effects=True, vmem_limit_bytes=VMEM_LIMIT),
        name="halo",
    )(velocity)


def band_matrix():
    taps = np.array([1, 2, 3, 4, 5, 4, 3, 2, 1], np.float32)
    center = np.zeros((128, 128), np.float32)
    edge = np.zeros((128, 128), np.float32)
    for source in range(128):
        for k in range(9):
            target = source + k - 4
            if 0 <= target < 128:
                center[source, target] = taps[k]
            else:
                edge[source, target % 128] = taps[k]
    half = np.concatenate([center, edge], axis=1)
    return np.concatenate([half, half], axis=0)


SCALE = 1.0 / 15625.0


def x_filter(flat, band, scale):
    high = flat.astype(jnp.bfloat16)
    low = (flat - high.astype(jnp.float32)).astype(jnp.bfloat16)
    both = jnp.dot(jnp.concatenate([high, low], axis=1), band, preferred_element_type=jnp.float32)
    center, edge = both[:, :128], both[:, 128:]
    lane = lax.broadcasted_iota(jnp.int32, flat.shape, 1)
    from_low = jnp.concatenate([edge[-DY:], edge[:-DY]], axis=0)
    from_high = jnp.concatenate([edge[DY:], edge[:DY]], axis=0)
    return (center + jnp.where(lane < 64, from_low, from_high)) * scale


def finish_kernel(rows, cols, nt, band, fp, fv, leonard, model, sums, bar, filtered):
    s = pl.program_id(0)
    shape = (DY, 128)
    lane = lax.broadcasted_iota(jnp.int32, shape, 1)
    line = lax.broadcasted_iota(jnp.int32, shape, 0)

    @pl.when(s == 0)
    def _():
        sums[...] = jnp.zeros_like(sums)

    r, c = lax.axis_index("row"), lax.axis_index("col")
    outside = jnp.logical_or(jnp.logical_and(s == 0, c == 0), jnp.logical_and(s == DZ + 1, c == cols - 1))
    keep = jnp.where(outside, 0.0, SCALE)
    for i in range(3):
        bar[i, s, 0] = x_filter(fv[i, 0, 0], band[...], keep)

    @pl.when(jnp.logical_and(s >= 1, s <= DZ))
    def _():
        below, above = jnp.where(r < rows - 1, 1.0, 0.0), jnp.where(r > 0, 1.0, 0.0)
        beyond = jnp.where(lax.broadcasted_iota(jnp.int32, (nt, DY, 128), 1) == 0, below, above).reshape(nt * DY, 128)
        for i in range(3):
            bar[i, s, 1] = x_filter(fv[i, 0, 1], band[...], SCALE) * beyond

    @pl.when(s >= 2)
    def _():
        k = s - 1

        for n in range(12):
            filtered[n] = x_filter(fp[n, 0], band[...], SCALE)

        @pl.loop(0, nt, step=8, init_carry=(jnp.zeros(shape, jnp.float32),) * 2)
        def totals(x0, carry):
            numer, denom = carry
            for x in range(8):
                x = x0 + x
                before, after = lax.rem(x + nt - 1, nt), lax.rem(x + 1, nt)
                at = lambda i, plane, x, part=0: bar[i, plane, part, pl.ds(pl.multiple_of(x * DY, DY), DY), :]
                u = [at(i, k, x) for i in range(3)]
                grads = []
                for i in range(3):
                    right = pltpu.roll(jnp.where(lane == 0, at(i, k, after), u[i]), 127, 1)
                    left = pltpu.roll(jnp.where(lane == 127, at(i, k, before), u[i]), 1, 1)
                    rim = at(i, k, x, 1)
                    down = pltpu.roll(jnp.where(line == 0, rim, u[i]), DY - 1, 0)
                    up = pltpu.roll(jnp.where(line == DY - 1, rim, u[i]), 1, 0)
                    grads.append([right - left, down - up, at(i, k + 1, x) - at(i, k - 1, x)])
                strain, quarter = strain_scaled(grads)
                scaled = 8.0 * quarter
                here = pl.ds(pl.multiple_of(x * DY, DY), DY)
                lanes = pl.ds(pl.multiple_of(x * 128, 128), 128)
                for n, (i, j) in enumerate(pair_list):
                    leonard_p = filtered[n, here, :] - u[i] * u[j]
                    model_p = 2.0 * filtered[6 + n, here, :] - scaled * strain[n]
                    leonard[n, 0, :, lanes] = leonard_p
                    model[n, 0, :, lanes] = model_p
                    weighted = model_p if pair_weight[n] == 1.0 else 2.0 * model_p
                    numer = numer + weighted * leonard_p
                    denom = denom + weighted * model_p
            return numer, denom

        sums[0] += totals[0]
        sums[1] += totals[1]


def finish(fp, fv, rows, cols, width):
    nt = width // 128
    f32 = functools.partial(jax.ShapeDtypeStruct, dtype=jnp.float32)
    scratch = lambda *shape: pltpu.VMEM((*shape, 128), jnp.float32)
    plane = lambda s: (0, jnp.maximum(s - 2, 0), 0, 0)
    return pl.pallas_call(
        functools.partial(finish_kernel, rows, cols, nt),
        grid=(DZ + 2,),
        out_shape=(f32((6, DZ, DY, width)), f32((6, DZ, DY, width)), f32((2, DY, 128))),
        in_specs=[
            pl.BlockSpec((256, 256), lambda s: (0, 0)),
            pl.BlockSpec((12, 1, nt * DY, 128), plane),
            pl.BlockSpec((3, 1, 2, nt * DY, 128), lambda s: (0, s, 0, 0, 0)),
        ],
        out_specs=(
            pl.BlockSpec((6, 1, DY, width), plane),
            pl.BlockSpec((6, 1, DY, width), plane),
            pl.BlockSpec((2, DY, 128), lambda s: (0, 0, 0)),
        ),
        scratch_shapes=[scratch(3, DZ + 2, 2, nt * DY), scratch(12, nt * DY)],
        compiler_params=pltpu.CompilerParams(vmem_limit_bytes=VMEM_LIMIT),
        name="finish",
    )(jnp.asarray(band_matrix(), jnp.bfloat16), fp, fv)


def total_kernel(cols, points, sums, coeff, own, parts, own_sem, send, recv):
    r = lax.axis_index("row")
    c = lax.axis_index("col")
    load = pltpu.make_async_copy(sums, own, own_sem)
    load.start()
    barrier = pltpu.get_barrier_semaphore()
    for step in range(1, cols):
        pl.semaphore_signal(barrier, inc=1, device_id=(r, lax.rem(c + step, cols)), device_id_type=MESH)
    pl.semaphore_wait(barrier, cols - 1)
    copies = [
        pltpu.make_async_remote_copy(
            src_ref=sums,
            dst_ref=parts.at[step - 1],
            send_sem=send.at[step - 1],
            recv_sem=recv.at[step - 1],
            device_id=(r, lax.rem(c + step, cols)),
            device_id_type=MESH,
        )
        for step in range(1, cols)
    ]
    for one in copies:
        one.start()
    load.wait()
    added = own[...]
    for step, one in enumerate(copies):
        one.wait_recv()
        added = added + parts[step]
    numer = jnp.sum(added[0], axis=1, keepdims=True) / points
    denom = jnp.sum(added[1], axis=1, keepdims=True) / points
    ratio = jnp.maximum(numer / (denom + 1e-06), 0.0)
    coeff[...] = -2.0 * ratio
    for one in copies:
        one.wait_send()


def total(sums, cols, points):
    in_vmem = pl.BlockSpec(memory_space=VMEM)
    dma = pltpu.SemaphoreType.DMA
    return pl.pallas_call(
        functools.partial(total_kernel, cols, points),
        out_shape=jax.ShapeDtypeStruct((DY, 1), jnp.float32),
        in_specs=[pl.BlockSpec(memory_space=pl.ANY)],
        out_specs=in_vmem,
        scratch_shapes=[pltpu.VMEM((2, DY, 128), jnp.float32), pltpu.VMEM((cols - 1, 2, DY, 128), jnp.float32), dma, dma((cols - 1,)), dma((cols - 1,))],
        compiler_params=pltpu.CompilerParams(collective_id=1, has_side_effects=True),
        name="total",
    )(sums)


def on_device(velocity):
    rows, cols = lax.axis_size("row"), lax.axis_size("col")
    width = velocity.shape[-1]
    fp, fv, ms = halo(velocity, rows, cols)
    leonard, model, sums = finish(fp, fv, rows, cols, width)
    coeff = total(sums, cols, width * DZ * cols)
    return leonard, model, ms * coeff[None, None]


def solution(mesh):
    placed = P(None, "col", "row", None)
    return jax.shard_map(on_device, mesh=mesh, in_specs=(placed,), out_specs=(placed, placed, placed), check_vma=False)
```

```python
import functools

import jax
import jax.numpy as jnp
import numpy as np
from jax import lax
from jax.experimental import pallas as pl
from jax.experimental.pallas import tpu as pltpu
from jax.sharding import PartitionSpec as P

MESH = pl.DeviceIdType.MESH
VMEM = pltpu.MemorySpace.VMEM
pair_list = ((0, 0), (0, 1), (0, 2), (1, 1), (1, 2), (2, 2))
pair_weight = (1.0, 2.0, 2.0, 1.0, 2.0, 1.0)

DZ = 4
DY = 8
H = 5
EZ = DZ + 2 * H
EY = DY + 2 * H
VMEM_LIMIT = 60 * 1024 * 1024
FIRST = (("y0", "z0", "r2", "y1", "r3", "y2", "y3", "s0", "p0"), ("z1", "s1", "p1", "z2", "s2", "p2", "z3", "s3", "p3", "f0"))
LATER = (("f1", "h0"), ("f2", "h1"), ("f3", "h2"), ("h3",))


def shifted(u, by):
    nt = u.shape[0]
    lane = lax.broadcasted_iota(jnp.int32, u.shape, 1)
    if by == 1:
        near = pltpu.roll(u, 127, 1)
        return jnp.where(lane == 127, pltpu.roll(near, nt - 1, 0), near)
    near = pltpu.roll(u, 1, 1)
    return jnp.where(lane == 0, pltpu.roll(near, 1, 0), near)


def double_box(cells):
    for _ in range(2):
        two = [a + b for a, b in zip(cells, cells[1:])]
        four = [a + b for a, b in zip(two, two[2:])]
        cells = [a + b for a, b in zip(four, cells[4:])]
    return cells


def strain_scaled(grads):
    diag = [grads[i][i] for i in range(3)]
    off = [grads[i][j] + grads[j][i] for i, j in ((0, 1), (0, 2), (1, 2))]
    total = 2.0 * (diag[0] * diag[0] + diag[1] * diag[1] + diag[2] * diag[2])
    total = total + (off[0] * off[0] + off[1] * off[1] + off[2] * off[2])
    quarter = jnp.sqrt(total * (1.0 / 64.0))
    diag = [d + d for d in diag]
    return (diag[0], off[0], off[1], diag[1], off[2], diag[2]), quarter


def halo_kernel(rows, cols, nt, vel_in, fp_out, fv_out, ms_out, vel, e, t, msr, turn, zp, zv, fp, fv, ms, z_send, z_recv, y_send, y_recv, s_send, s_recv, o_sem, v_sem):
    load = pltpu.make_async_copy(vel_in, vel, v_sem)
    load.start()
    groups = nt // 8
    cuts = [7] + [17 + 8 * g for g in range(groups - 1)] + [7 + nt]
    r = lax.axis_index("row")
    c = lax.axis_index("col")
    odd = lax.rem(c, 2)
    out = 2 * odd - 1
    sibling = c - out
    outer1, outer2, inner2 = c + out, c + 2 * out, c - 2 * out
    has_outer = jnp.logical_and(outer1 >= 0, outer1 < cols)
    has_inner2 = jnp.logical_and(inner2 >= 0, inner2 < cols)
    place = lax.rem(r, 4)
    helps = jnp.logical_and(jnp.logical_or(place == 1, place == 2), has_outer)
    helped = jnp.logical_and(jnp.logical_or(place == 0, place == 3), has_outer)
    mate = r + 1 - 2 * lax.rem(r, 2)
    has_up = r > 0
    has_down = r < rows - 1

    barrier = pltpu.get_barrier_semaphore()
    partners = (
        (has_up, r - 1, c),
        (has_down, r + 1, c),
        (c >= 0, r, sibling),
        (has_outer, r, outer1),
        (has_outer, r, outer2),
        (has_inner2, r, inner2),
        (has_outer, mate, outer1),
    )
    count = 0
    for there, row, col in partners:

        @pl.when(there)
        def _(row=row, col=col):
            pl.semaphore_signal(barrier, inc=1, device_id=(row, col), device_id_type=MESH)

        count = count + there.astype(jnp.int32)

    def relay(g):
        @pl.loop(0, 3)
        def _(i):
            for k in range(DZ):
                own_rows = vel[i, k, :, g * 1024 : (g + 1) * 1024].reshape(DY, 8, 128)
                e[i, H + k, H : H + DY, 8 + 8 * g : 16 + 8 * g, :] = own_rows

    load.wait()
    for g in range(min(2, groups)):
        relay(g)

    @pl.loop(0, 3)
    def _(i):
        for k in range(DZ):
            e[i, H + k, H : H + DY, 7:8, :] = vel[i, k, :, (nt - 1) * 128 :].reshape(DY, 1, 128)

    zero = jnp.zeros((nt + 16, 128), jnp.float32)
    mine = H * odd

    def clear(plane0, planes, row0, count_rows):
        @pl.loop(0, 3 * planes * count_rows)
        def _(n):
            i, rest = n // (planes * count_rows), lax.rem(n, planes * count_rows)
            e[i, plane0 + rest // count_rows, row0 + lax.rem(rest, count_rows)] = zero

    @pl.when(jnp.logical_not(has_up))
    def _():
        clear(mine, EZ - H, 0, H)

    @pl.when(jnp.logical_not(has_down))
    def _():
        clear(mine, EZ - H, H + DY, H)

    @pl.when(jnp.logical_not(has_outer))
    def _():
        clear(odd * (H + DZ), H, 0, EY)

    pl.semaphore_wait(barrier, count)

    def copy(g, p_src, p_dst, planes, q_src, q_dst, count_rows, send, recv, row, col):
        tiles = pl.ds(cuts[g], cuts[g + 1] - cuts[g])
        return pltpu.make_async_remote_copy(
            src_ref=e.at[:, pl.ds(p_src, planes), pl.ds(q_src, count_rows), tiles],
            dst_ref=e.at[:, pl.ds(p_dst, planes), pl.ds(q_dst, count_rows), tiles],
            send_sem=send,
            recv_sem=recv,
            device_id=(row, col),
            device_id_type=MESH,
        )

    own = H
    far = odd * (H + DZ)
    near = 4 + 5 * odd

    def z_copies(g):
        single = copy(g, 8 - 3 * odd, 13 * odd, 1, H, H, DY, z_send.at[g, 0], z_recv.at[g, 0], r, inner2)
        whole = copy(g, own, 9 - 8 * odd, DZ, H, H, DY, z_send.at[g, 1], z_recv.at[g, 1], r, outer1)
        row = jnp.where(place == 0, H, H + 5)
        part = copy(g, own, 9 - 8 * odd, DZ, row, row, DY - H, z_send.at[g, 2], z_recv.at[g, 2], r, outer1)
        return (helped, part, helped), (helps, whole, helps), (has_inner2, single, has_outer)

    def proxy_copies(g):
        low = place < 2
        src, dst = jnp.where(low, 0, H + DY), jnp.where(low, DY, H)
        one = copy(g, own, 9 - 8 * odd, DZ, src, dst, H, z_send.at[g, 3], z_recv.at[g, 3], mate, outer1)
        return ((helps, one, helped),)

    def y_copies(g, kind):
        plane, planes = ((own, DZ), (far, H))[kind]
        on = jnp.logical_or(kind == 0, has_outer)
        up_there, down_there = jnp.logical_and(has_up, on), jnp.logical_and(has_down, on)
        up = copy(g, plane, plane, planes, H, H + DY, H, y_send.at[g, 0, kind], y_recv.at[g, 0, kind], r - 1, c)
        down = copy(g, plane, plane, planes, DY, 0, H, y_send.at[g, 1, kind], y_recv.at[g, 1, kind], r + 1, c)
        return (up_there, up, down_there), (down_there, down, up_there)

    def s_copies(g):
        dst = 1 + 8 * odd
        yes = c >= 0
        plan = ((own, dst, DZ, H, DY), (own, dst, DZ, 0, H), (own, dst, DZ, H + DY, H))
        plan = plan + tuple((near, 13 * odd, 1, q, n) for _, _, _, q, n in plan)
        return [
            (yes, copy(g, src, to, planes, q, q, n, s_send.at[g, m], s_recv.at[g, m], r, sibling), yes)
            for m, (src, to, planes, q, n) in enumerate(plan)
        ]

    def start(copies):
        for sends, one, _ in copies:
            pl.when(sends)(one.start)

    def wait_recv(copies):
        for _, one, receives in copies:
            pl.when(receives)(one.wait_recv)

    def wait_send(copies):
        for sends, one, _ in copies:
            pl.when(sends)(one.wait_send)

    def proxy(g):
        wait_recv(y_copies(g, 0))
        start(proxy_copies(g))
        start(s_copies(g)[1:3])

    def forward(g):
        wait_recv(z_copies(g))
        wait_recv(proxy_copies(g))
        start(y_copies(g, 1))
        start(s_copies(g)[3:4])

    def share(g):
        wait_recv(y_copies(g, 1))
        start(s_copies(g)[4:])

    acts = {
        "r": relay,
        "z": lambda g: start(z_copies(g)),
        "y": lambda g: start(y_copies(g, 0)),
        "s": lambda g: start(s_copies(g)[:1]),
        "p": proxy,
        "f": forward,
        "h": share,
    }

    def run(plan):
        for act in plan:
            if int(act[1]) < groups:
                acts[act[0]](int(act[1]))

    for plan in FIRST:
        run(plan)

    y_first = r * DY - 4
    z_first = c * DZ - 4

    def results(x):
        tiles = pl.ds(x * DY if isinstance(x, int) else pl.multiple_of(x * DY, 64), 8 * DY)
        lanes = pl.ds(x * 128 if isinstance(x, int) else pl.multiple_of(x * 128, 1024), 1024)
        g = x // 8
        return (
            pltpu.make_async_copy(fp.at[:, :, tiles], fp_out.at[:, :, tiles], o_sem.at[g, 0]),
            pltpu.make_async_copy(fv.at[:, :, :, tiles], fv_out.at[:, :, :, tiles], o_sem.at[g, 1]),
            pltpu.make_async_copy(ms.at[:, :, :, lanes], ms_out.at[:, :, :, lanes], o_sem.at[g, 2]),
        )

    lane = lax.broadcasted_iota(jnp.int32, (8, 128), 1)

    def compute(x, rest):
        at = pl.ds(pl.multiple_of(8 + x, 8), 8)
        before, after = pl.ds(7 + x, 8), pl.ds(9 + x, 8)
        to = pl.ds(pl.multiple_of(x, 8), 8)

        @pl.loop(6 * rest, 6 + 10 * rest)
        def _(m):
            q = jnp.where(m < 6, m + 5, jnp.where(m < 11, m - 6, m))
            in_y = jnp.where(jnp.logical_and(y_first + q >= 0, y_first + q < rows * DY), 1.0, 0.0)
            for p in range(EZ - 2):
                grads = []
                for i in range(3):
                    u = e[i, p + 1, q + 1, at, :]
                    right = pltpu.roll(jnp.where(lane == 0, e[i, p + 1, q + 1, after, :], u), 127, 1)
                    left = pltpu.roll(jnp.where(lane == 127, e[i, p + 1, q + 1, before, :], u), 1, 1)
                    grads.append(
                        [
                            right - left,
                            e[i, p + 1, q + 2, at, :] - e[i, p + 1, q, at, :],
                            e[i, p + 2, q + 1, at, :] - e[i, p, q + 1, at, :],
                        ]
                    )
                strain, quarter = strain_scaled(grads)
                in_z = jnp.logical_and(z_first + p >= 0, z_first + p < cols * DZ)
                quarter = quarter * jnp.where(in_z, in_y, 0.0)
                for n in range(6):
                    value = quarter * strain[n]
                    t[n, p] = value
                    if 4 <= p < 4 + DZ:
                        msr[n, p - 4, pl.ds(pl.multiple_of(q * 8, 8), 8), :] = value
            for n, (i, j) in enumerate(pair_list):
                cells = [e[i, p, q + 1, at, :] * e[j, p, q + 1, at, :] for p in range(1, EZ - 1)]
                for k, value in enumerate(double_box(cells)):
                    zp[n, k, q] = value
                for k, value in enumerate(double_box([t[n, p] for p in range(EZ - 2)])):
                    zp[6 + n, k, q] = value

        @pl.loop(DY * rest, DY + 2 * H * rest)
        def _(m):
            q = jnp.where(m < DY, m + H, jnp.where(m < DY + H, m - DY, m))
            for i in range(3):
                for k, value in enumerate(double_box([e[i, p, q, at, :] for p in range(EZ)])):
                    zv[i, k, q] = value

        @pl.when(rest == 1)
        def _():
            @pl.loop(0, 6)
            def _(n):
                for k in range(DZ):
                    for j in range(8):
                        ms[n, k, :, pl.ds(pl.multiple_of((x + j) * 128, 128), 128)] = msr[n, k, pl.ds(4 * 8 + j, DY, stride=8), :]

            def turned(slot, dst, values):
                for y, value in enumerate(values):
                    turn[slot, y * 8 : (y + 1) * 8, :] = value
                for j in range(8):
                    dst[pl.ds(pl.multiple_of((x + j) * DY, DY), DY), :] = turn[slot, pl.ds(j, DY, stride=8), :]

            @pl.loop(0, 12)
            def _(f):
                for k in range(DZ):
                    turned(k, fp.at[f, k], double_box([zp[f, k, q] for q in range(EY - 2)]))

            @pl.loop(0, DZ + 2)
            def _(k):
                for i in range(3):
                    values = double_box([zv[i, k, q] for q in range(EY)])
                    turned(2 * i, fv.at[i, k, 0], values[1 : DY + 1])
                    turned(2 * i + 1, fv.at[i, k, 1], [values[DY + 1]] + [values[0]] * (DY - 1))

            for one in results(x):
                one.start()

    @pl.loop(0, 2 * groups)
    def _(turn_of):
        g, rest = turn_of // 2, lax.rem(turn_of, 2)
        for step in range(groups):

            @pl.when(turn_of == 2 * step)
            def _(step=step):
                wait_recv(s_copies(step)[0:4:3])
                if step == groups - 1:

                    @pl.loop(0, 3 * EZ)
                    def _(n):
                        i, p = n // EZ, lax.rem(n, EZ)
                        e[i, p, :, 7 + nt : 9 + nt, :] = e[i, p, :, 7:9, :]

            @pl.when(turn_of == 2 * step + 1)
            def _(step=step):
                wait_recv(s_copies(step)[1:3])
                wait_recv(s_copies(step)[4:])

        compute(g * 8, rest)
        for step in range(groups):

            @pl.when(turn_of == 2 * step)
            def _(step=step):
                run(LATER[step])

    for g in range(groups):
        for one in results(8 * g):
            one.wait()
        wait_send(z_copies(g))
        wait_send(proxy_copies(g))
        wait_send(y_copies(g, 0))
        wait_send(y_copies(g, 1))
        wait_send(s_copies(g))


def halo(velocity, rows, cols):
    nt = velocity.shape[-1] // 128
    groups = nt // 8
    f32 = functools.partial(jax.ShapeDtypeStruct, dtype=jnp.float32)
    in_hbm = pl.BlockSpec(memory_space=pl.ANY)
    dma = pltpu.SemaphoreType.DMA
    scratch = lambda *shape: pltpu.VMEM((*shape, 128), jnp.float32)
    return pl.pallas_call(
        functools.partial(halo_kernel, rows, cols, nt),
        out_shape=(f32((12, DZ, nt * DY, 128)), f32((3, DZ + 2, 2, nt * DY, 128)), f32((6, DZ, DY, nt * 128))),
        in_specs=[in_hbm],
        out_specs=(in_hbm, in_hbm, in_hbm),
        scratch_shapes=[
            pltpu.VMEM(velocity.shape, jnp.float32),
            scratch(3, EZ, EY, nt + 16),
            scratch(6, EZ - 2, 8),
            scratch(6, DZ, (EY - 2) * 8),
            scratch(6, 8 * DY),
            scratch(12, DZ, EY - 2, 8),
            scratch(3, DZ + 2, EY, 8),
            scratch(12, DZ, nt * DY),
            scratch(3, DZ + 2, 2, nt * DY),
            pltpu.VMEM((6, DZ, DY, nt * 128), jnp.float32),
            dma((groups, 4)),
            dma((groups, 4)),
            dma((groups, 2, 2)),
            dma((groups, 2, 2)),
            dma((groups, 6)),
            dma((groups, 6)),
            dma((groups, 3)),
            dma,
        ],
        compiler_params=pltpu.CompilerParams(collective_id=0, has_side_effects=True, vmem_limit_bytes=VMEM_LIMIT),
        name="halo",
    )(velocity)


def band_matrix():
    taps = np.array([1, 2, 3, 4, 5, 4, 3, 2, 1], np.float32)
    center = np.zeros((128, 128), np.float32)
    edge = np.zeros((128, 128), np.float32)
    for source in range(128):
        for k in range(9):
            target = source + k - 4
            if 0 <= target < 128:
                center[source, target] = taps[k]
            else:
                edge[source, target % 128] = taps[k]
    half = np.concatenate([center, edge], axis=1)
    return np.concatenate([half, half], axis=0)


SCALE = 1.0 / 15625.0


def x_filter(flat, band, scale):
    high = flat.astype(jnp.bfloat16)
    low = (flat - high.astype(jnp.float32)).astype(jnp.bfloat16)
    both = jnp.dot(jnp.concatenate([high, low], axis=1), band, preferred_element_type=jnp.float32)
    center, edge = both[:, :128], both[:, 128:]
    lane = lax.broadcasted_iota(jnp.int32, flat.shape, 1)
    from_low = jnp.concatenate([edge[-DY:], edge[:-DY]], axis=0)
    from_high = jnp.concatenate([edge[DY:], edge[:DY]], axis=0)
    return (center + jnp.where(lane < 64, from_low, from_high)) * scale


def finish_kernel(rows, cols, nt, band, fp, fv, leonard, model, sums, bar, filtered):
    s = pl.program_id(0)
    shape = (DY, 128)
    lane = lax.broadcasted_iota(jnp.int32, shape, 1)
    line = lax.broadcasted_iota(jnp.int32, shape, 0)

    @pl.when(s == 0)
    def _():
        sums[...] = jnp.zeros_like(sums)

    r, c = lax.axis_index("row"), lax.axis_index("col")
    outside = jnp.logical_or(jnp.logical_and(s == 0, c == 0), jnp.logical_and(s == DZ + 1, c == cols - 1))
    keep = jnp.where(outside, 0.0, SCALE)
    for i in range(3):
        bar[i, s, 0] = x_filter(fv[i, 0, 0], band[...], keep)

    @pl.when(jnp.logical_and(s >= 1, s <= DZ))
    def _():
        below, above = jnp.where(r < rows - 1, 1.0, 0.0), jnp.where(r > 0, 1.0, 0.0)
        beyond = jnp.where(lax.broadcasted_iota(jnp.int32, (nt, DY, 128), 1) == 0, below, above).reshape(nt * DY, 128)
        for i in range(3):
            bar[i, s, 1] = x_filter(fv[i, 0, 1], band[...], SCALE) * beyond

    @pl.when(s >= 2)
    def _():
        k = s - 1

        for n in range(12):
            filtered[n] = x_filter(fp[n, 0], band[...], SCALE)

        @pl.loop(0, nt, step=32, init_carry=(jnp.zeros(shape, jnp.float32),) * 2)
        def totals(x0, carry):
            numer, denom = carry
            for x in range(32):
                x = x0 + x
                before, after = lax.rem(x + nt - 1, nt), lax.rem(x + 1, nt)
                at = lambda i, plane, x, part=0: bar[i, plane, part, pl.ds(pl.multiple_of(x * DY, DY), DY), :]
                u = [at(i, k, x) for i in range(3)]
                grads = []
                for i in range(3):
                    right = pltpu.roll(jnp.where(lane == 0, at(i, k, after), u[i]), 127, 1)
                    left = pltpu.roll(jnp.where(lane == 127, at(i, k, before), u[i]), 1, 1)
                    rim = at(i, k, x, 1)
                    down = pltpu.roll(jnp.where(line == 0, rim, u[i]), DY - 1, 0)
                    up = pltpu.roll(jnp.where(line == DY - 1, rim, u[i]), 1, 0)
                    grads.append([right - left, down - up, at(i, k + 1, x) - at(i, k - 1, x)])
                strain, quarter = strain_scaled(grads)
                scaled = 8.0 * quarter
                here = pl.ds(pl.multiple_of(x * DY, DY), DY)
                lanes = pl.ds(pl.multiple_of(x * 128, 128), 128)
                for n, (i, j) in enumerate(pair_list):
                    leonard_p = filtered[n, here, :] - u[i] * u[j]
                    model_p = 2.0 * filtered[6 + n, here, :] - scaled * strain[n]
                    leonard[n, 0, :, lanes] = leonard_p
                    model[n, 0, :, lanes] = model_p
                    weighted = model_p if pair_weight[n] == 1.0 else 2.0 * model_p
                    numer = numer + weighted * leonard_p
                    denom = denom + weighted * model_p
            return numer, denom

        sums[0] += totals[0]
        sums[1] += totals[1]


def finish(fp, fv, rows, cols, width):
    nt = width // 128
    f32 = functools.partial(jax.ShapeDtypeStruct, dtype=jnp.float32)
    scratch = lambda *shape: pltpu.VMEM((*shape, 128), jnp.float32)
    plane = lambda s: (0, jnp.maximum(s - 2, 0), 0, 0)
    return pl.pallas_call(
        functools.partial(finish_kernel, rows, cols, nt),
        grid=(DZ + 2,),
        out_shape=(f32((6, DZ, DY, width)), f32((6, DZ, DY, width)), f32((2, DY, 128))),
        in_specs=[
            pl.BlockSpec((256, 256), lambda s: (0, 0)),
            pl.BlockSpec((12, 1, nt * DY, 128), plane),
            pl.BlockSpec((3, 1, 2, nt * DY, 128), lambda s: (0, s, 0, 0, 0)),
        ],
        out_specs=(
            pl.BlockSpec((6, 1, DY, width), plane),
            pl.BlockSpec((6, 1, DY, width), plane),
            pl.BlockSpec((2, DY, 128), lambda s: (0, 0, 0)),
        ),
        scratch_shapes=[scratch(3, DZ + 2, 2, nt * DY), scratch(12, nt * DY)],
        compiler_params=pltpu.CompilerParams(vmem_limit_bytes=VMEM_LIMIT),
        name="finish",
    )(jnp.asarray(band_matrix(), jnp.bfloat16), fp, fv)


def total_kernel(cols, points, sums, coeff, own, parts, own_sem, send, recv):
    r = lax.axis_index("row")
    c = lax.axis_index("col")
    load = pltpu.make_async_copy(sums, own, own_sem)
    load.start()
    barrier = pltpu.get_barrier_semaphore()
    for step in range(1, cols):
        pl.semaphore_signal(barrier, inc=1, device_id=(r, lax.rem(c + step, cols)), device_id_type=MESH)
    pl.semaphore_wait(barrier, cols - 1)
    copies = [
        pltpu.make_async_remote_copy(
            src_ref=sums,
            dst_ref=parts.at[step - 1],
            send_sem=send.at[step - 1],
            recv_sem=recv.at[step - 1],
            device_id=(r, lax.rem(c + step, cols)),
            device_id_type=MESH,
        )
        for step in range(1, cols)
    ]
    for one in copies:
        one.start()
    load.wait()
    added = own[...]
    for step, one in enumerate(copies):
        one.wait_recv()
        added = added + parts[step]
    numer = jnp.sum(added[0], axis=1, keepdims=True) / points
    denom = jnp.sum(added[1], axis=1, keepdims=True) / points
    ratio = jnp.maximum(numer / (denom + 1e-06), 0.0)
    coeff[...] = jnp.broadcast_to(-2.0 * ratio, coeff.shape)
    for one in copies:
        one.wait_send()


def total(sums, cols, width):
    in_vmem = pl.BlockSpec(memory_space=VMEM)
    dma = pltpu.SemaphoreType.DMA
    return pl.pallas_call(
        functools.partial(total_kernel, cols, width * DZ * cols),
        out_shape=jax.ShapeDtypeStruct((DY, width), jnp.float32),
        in_specs=[pl.BlockSpec(memory_space=pl.ANY)],
        out_specs=in_vmem,
        scratch_shapes=[pltpu.VMEM((2, DY, 128), jnp.float32), pltpu.VMEM((cols - 1, 2, DY, 128), jnp.float32), dma, dma((cols - 1,)), dma((cols - 1,))],
        compiler_params=pltpu.CompilerParams(collective_id=1, has_side_effects=True),
        name="total",
    )(sums)


def on_device(velocity):
    rows, cols = lax.axis_size("row"), lax.axis_size("col")
    width = velocity.shape[-1]
    fp, fv, ms = halo(velocity, rows, cols)
    leonard, model, sums = finish(fp, fv, rows, cols, width)
    coeff = total(sums, cols, width)
    return leonard, model, ms * coeff[None, None]


def solution(mesh):
    placed = P(None, "col", "row", None)
    return jax.shard_map(on_device, mesh=mesh, in_specs=(placed,), out_specs=(placed, placed, placed), check_vma=False)
```

```python
import functools

import jax
import jax.numpy as jnp
import numpy as np
from jax import lax
from jax.experimental import pallas as pl
from jax.experimental.pallas import tpu as pltpu
from jax.sharding import PartitionSpec as P

MESH = pl.DeviceIdType.MESH
VMEM = pltpu.MemorySpace.VMEM
pair_list = ((0, 0), (0, 1), (0, 2), (1, 1), (1, 2), (2, 2))
pair_weight = (1.0, 2.0, 2.0, 1.0, 2.0, 1.0)

DZ = 4
DY = 8
H = 5
EZ = DZ + 2 * H
EY = DY + 2 * H
VMEM_LIMIT = 60 * 1024 * 1024
FIRST = (("y0", "z0", "r2", "y1", "r3", "y2", "y3", "s0", "p0", "z1"), ("s1", "p1", "z2", "s2", "p2", "z3", "s3", "p3", "f0", "f1"))
LATER = (("h0",), ("f2", "h1"), ("f3", "h2"), ("h3",))


def shifted(u, by):
    nt = u.shape[0]
    lane = lax.broadcasted_iota(jnp.int32, u.shape, 1)
    if by == 1:
        near = pltpu.roll(u, 127, 1)
        return jnp.where(lane == 127, pltpu.roll(near, nt - 1, 0), near)
    near = pltpu.roll(u, 1, 1)
    return jnp.where(lane == 0, pltpu.roll(near, 1, 0), near)


def double_box(cells):
    for _ in range(2):
        two = [a + b for a, b in zip(cells, cells[1:])]
        four = [a + b for a, b in zip(two, two[2:])]
        cells = [a + b for a, b in zip(four, cells[4:])]
    return cells


def strain_scaled(grads):
    diag = [grads[i][i] for i in range(3)]
    off = [grads[i][j] + grads[j][i] for i, j in ((0, 1), (0, 2), (1, 2))]
    total = 2.0 * (diag[0] * diag[0] + diag[1] * diag[1] + diag[2] * diag[2])
    total = total + (off[0] * off[0] + off[1] * off[1] + off[2] * off[2])
    quarter = jnp.sqrt(total * (1.0 / 64.0))
    diag = [d + d for d in diag]
    return (diag[0], off[0], off[1], diag[1], off[2], diag[2]), quarter


def halo_kernel(rows, cols, nt, vel_in, fp_out, fv_out, ms_out, vel, e, t, msr, turn, zp, zv, fp, fv, ms, z_send, z_recv, y_send, y_recv, s_send, s_recv, o_sem, v_sem):
    load = pltpu.make_async_copy(vel_in, vel, v_sem)
    load.start()
    groups = nt // 8
    cuts = [7] + [17 + 8 * g for g in range(groups - 1)] + [7 + nt]
    r = lax.axis_index("row")
    c = lax.axis_index("col")
    odd = lax.rem(c, 2)
    out = 2 * odd - 1
    sibling = c - out
    outer1, outer2, inner2 = c + out, c + 2 * out, c - 2 * out
    has_outer = jnp.logical_and(outer1 >= 0, outer1 < cols)
    has_inner2 = jnp.logical_and(inner2 >= 0, inner2 < cols)
    place = lax.rem(r, 4)
    helps = jnp.logical_and(jnp.logical_or(place == 1, place == 2), has_outer)
    helped = jnp.logical_and(jnp.logical_or(place == 0, place == 3), has_outer)
    mate = r + 1 - 2 * lax.rem(r, 2)
    has_up = r > 0
    has_down = r < rows - 1

    barrier = pltpu.get_barrier_semaphore()
    partners = (
        (has_up, r - 1, c),
        (has_down, r + 1, c),
        (c >= 0, r, sibling),
        (has_outer, r, outer1),
        (has_outer, r, outer2),
        (has_inner2, r, inner2),
        (has_outer, mate, outer1),
    )
    count = 0
    for there, row, col in partners:

        @pl.when(there)
        def _(row=row, col=col):
            pl.semaphore_signal(barrier, inc=1, device_id=(row, col), device_id_type=MESH)

        count = count + there.astype(jnp.int32)

    def relay(g):
        @pl.loop(0, 3)
        def _(i):
            for k in range(DZ):
                own_rows = vel[i, k, :, g * 1024 : (g + 1) * 1024].reshape(DY, 8, 128)
                e[i, H + k, H : H + DY, 8 + 8 * g : 16 + 8 * g, :] = own_rows

    load.wait()
    for g in range(min(2, groups)):
        relay(g)

    @pl.loop(0, 3)
    def _(i):
        for k in range(DZ):
            e[i, H + k, H : H + DY, 7:8, :] = vel[i, k, :, (nt - 1) * 128 :].reshape(DY, 1, 128)

    zero = jnp.zeros((nt + 16, 128), jnp.float32)
    mine = H * odd

    def clear(plane0, planes, row0, count_rows):
        @pl.loop(0, 3 * planes * count_rows)
        def _(n):
            i, rest = n // (planes * count_rows), lax.rem(n, planes * count_rows)
            e[i, plane0 + rest // count_rows, row0 + lax.rem(rest, count_rows)] = zero

    @pl.when(jnp.logical_not(has_up))
    def _():
        clear(mine, EZ - H, 0, H)

    @pl.when(jnp.logical_not(has_down))
    def _():
        clear(mine, EZ - H, H + DY, H)

    @pl.when(jnp.logical_not(has_outer))
    def _():
        clear(odd * (H + DZ), H, 0, EY)

    pl.semaphore_wait(barrier, count)

    def copy(g, p_src, p_dst, planes, q_src, q_dst, count_rows, send, recv, row, col):
        tiles = pl.ds(cuts[g], cuts[g + 1] - cuts[g])
        return pltpu.make_async_remote_copy(
            src_ref=e.at[:, pl.ds(p_src, planes), pl.ds(q_src, count_rows), tiles],
            dst_ref=e.at[:, pl.ds(p_dst, planes), pl.ds(q_dst, count_rows), tiles],
            send_sem=send,
            recv_sem=recv,
            device_id=(row, col),
            device_id_type=MESH,
        )

    own = H
    far = odd * (H + DZ)
    near = 4 + 5 * odd

    def z_copies(g):
        single = copy(g, 8 - 3 * odd, 13 * odd, 1, H, H, DY, z_send.at[g, 0], z_recv.at[g, 0], r, inner2)
        whole = copy(g, own, 9 - 8 * odd, DZ, H, H, DY, z_send.at[g, 1], z_recv.at[g, 1], r, outer1)
        row = jnp.where(place == 0, H, H + 5)
        part = copy(g, own, 9 - 8 * odd, DZ, row, row, DY - H, z_send.at[g, 2], z_recv.at[g, 2], r, outer1)
        return (helped, part, helped), (helps, whole, helps), (has_inner2, single, has_outer)

    def proxy_copies(g):
        low = place < 2
        src, dst = jnp.where(low, 0, H + DY), jnp.where(low, DY, H)
        one = copy(g, own, 9 - 8 * odd, DZ, src, dst, H, z_send.at[g, 3], z_recv.at[g, 3], mate, outer1)
        return ((helps, one, helped),)

    def y_copies(g, kind):
        plane, planes = ((own, DZ), (far, H))[kind]
        on = jnp.logical_or(kind == 0, has_outer)
        up_there, down_there = jnp.logical_and(has_up, on), jnp.logical_and(has_down, on)
        up = copy(g, plane, plane, planes, H, H + DY, H, y_send.at[g, 0, kind], y_recv.at[g, 0, kind], r - 1, c)
        down = copy(g, plane, plane, planes, DY, 0, H, y_send.at[g, 1, kind], y_recv.at[g, 1, kind], r + 1, c)
        return (up_there, up, down_there), (down_there, down, up_there)

    def s_copies(g):
        dst = 1 + 8 * odd
        yes = c >= 0
        plan = ((own, dst, DZ, H, DY), (own, dst, DZ, 0, H), (own, dst, DZ, H + DY, H))
        plan = plan + tuple((near, 13 * odd, 1, q, n) for _, _, _, q, n in plan)
        return [
            (yes, copy(g, src, to, planes, q, q, n, s_send.at[g, m], s_recv.at[g, m], r, sibling), yes)
            for m, (src, to, planes, q, n) in enumerate(plan)
        ]

    def start(copies):
        for sends, one, _ in copies:
            pl.when(sends)(one.start)

    def wait_recv(copies):
        for _, one, receives in copies:
            pl.when(receives)(one.wait_recv)

    def wait_send(copies):
        for sends, one, _ in copies:
            pl.when(sends)(one.wait_send)

    def proxy(g):
        wait_recv(y_copies(g, 0))
        start(proxy_copies(g))
        start(s_copies(g)[1:3])

    def forward(g):
        wait_recv(z_copies(g))
        wait_recv(proxy_copies(g))
        start(y_copies(g, 1))
        start(s_copies(g)[3:4])

    def share(g):
        wait_recv(y_copies(g, 1))
        start(s_copies(g)[4:])

    acts = {
        "r": relay,
        "z": lambda g: start(z_copies(g)),
        "y": lambda g: start(y_copies(g, 0)),
        "s": lambda g: start(s_copies(g)[:1]),
        "p": proxy,
        "f": forward,
        "h": share,
    }

    def run(plan):
        for act in plan:
            if int(act[1]) < groups:
                acts[act[0]](int(act[1]))

    for plan in FIRST:
        run(plan)

    y_first = r * DY - 4
    z_first = c * DZ - 4

    def results(x):
        tiles = pl.ds(x * DY if isinstance(x, int) else pl.multiple_of(x * DY, 64), 8 * DY)
        lanes = pl.ds(x * 128 if isinstance(x, int) else pl.multiple_of(x * 128, 1024), 1024)
        g = x // 8
        return (
            pltpu.make_async_copy(fp.at[:, :, tiles], fp_out.at[:, :, tiles], o_sem.at[g, 0]),
            pltpu.make_async_copy(fv.at[:, :, :, tiles], fv_out.at[:, :, :, tiles], o_sem.at[g, 1]),
            pltpu.make_async_copy(ms.at[:, :, :, lanes], ms_out.at[:, :, :, lanes], o_sem.at[g, 2]),
        )

    lane = lax.broadcasted_iota(jnp.int32, (8, 128), 1)

    def compute(x, rest):
        at = pl.ds(pl.multiple_of(8 + x, 8), 8)
        before, after = pl.ds(7 + x, 8), pl.ds(9 + x, 8)
        to = pl.ds(pl.multiple_of(x, 8), 8)

        @pl.loop(6 * rest, 6 + 10 * rest)
        def _(m):
            q = jnp.where(m < 6, m + 5, jnp.where(m < 11, m - 6, m))
            in_y = jnp.where(jnp.logical_and(y_first + q >= 0, y_first + q < rows * DY), 1.0, 0.0)
            for p in range(EZ - 2):
                grads = []
                for i in range(3):
                    u = e[i, p + 1, q + 1, at, :]
                    right = pltpu.roll(jnp.where(lane == 0, e[i, p + 1, q + 1, after, :], u), 127, 1)
                    left = pltpu.roll(jnp.where(lane == 127, e[i, p + 1, q + 1, before, :], u), 1, 1)
                    grads.append(
                        [
                            right - left,
                            e[i, p + 1, q + 2, at, :] - e[i, p + 1, q, at, :],
                            e[i, p + 2, q + 1, at, :] - e[i, p, q + 1, at, :],
                        ]
                    )
                strain, quarter = strain_scaled(grads)
                in_z = jnp.logical_and(z_first + p >= 0, z_first + p < cols * DZ)
                quarter = quarter * jnp.where(in_z, in_y, 0.0)
                for n in range(6):
                    value = quarter * strain[n]
                    t[n, p] = value
                    if 4 <= p < 4 + DZ:
                        msr[n, p - 4, pl.ds(pl.multiple_of(q * 8, 8), 8), :] = value
            for n, (i, j) in enumerate(pair_list):
                cells = [e[i, p, q + 1, at, :] * e[j, p, q + 1, at, :] for p in range(1, EZ - 1)]
                for k, value in enumerate(double_box(cells)):
                    zp[n, k, q] = value
                for k, value in enumerate(double_box([t[n, p] for p in range(EZ - 2)])):
                    zp[6 + n, k, q] = value

        @pl.loop(DY * rest, DY + 2 * H * rest)
        def _(m):
            q = jnp.where(m < DY, m + H, jnp.where(m < DY + H, m - DY, m))
            for i in range(3):
                for k, value in enumerate(double_box([e[i, p, q, at, :] for p in range(EZ)])):
                    zv[i, k, q] = value

        @pl.when(rest == 1)
        def _():
            @pl.loop(0, 6)
            def _(n):
                for k in range(DZ):
                    for j in range(8):
                        ms[n, k, :, pl.ds(pl.multiple_of((x + j) * 128, 128), 128)] = msr[n, k, pl.ds(4 * 8 + j, DY, stride=8), :]

            def turned(slot, dst, values):
                for y, value in enumerate(values):
                    turn[slot, y * 8 : (y + 1) * 8, :] = value
                for j in range(8):
                    dst[pl.ds(pl.multiple_of((x + j) * DY, DY), DY), :] = turn[slot, pl.ds(j, DY, stride=8), :]

            @pl.loop(0, 12)
            def _(f):
                for k in range(DZ):
                    turned(k, fp.at[f, k], double_box([zp[f, k, q] for q in range(EY - 2)]))

            @pl.loop(0, DZ + 2)
            def _(k):
                for i in range(3):
                    values = double_box([zv[i, k, q] for q in range(EY)])
                    turned(2 * i, fv.at[i, k, 0], values[1 : DY + 1])
                    turned(2 * i + 1, fv.at[i, k, 1], [values[DY + 1]] + [values[0]] * (DY - 1))

            for one in results(x):
                one.start()

    @pl.loop(0, 2 * groups)
    def _(turn_of):
        g, rest = turn_of // 2, lax.rem(turn_of, 2)
        for step in range(groups):

            @pl.when(turn_of == 2 * step)
            def _(step=step):
                wait_recv(s_copies(step)[0:4:3])
                if step == groups - 1:

                    @pl.loop(0, 3 * EZ)
                    def _(n):
                        i, p = n // EZ, lax.rem(n, EZ)
                        e[i, p, :, 7 + nt : 9 + nt, :] = e[i, p, :, 7:9, :]

            @pl.when(turn_of == 2 * step + 1)
            def _(step=step):
                wait_recv(s_copies(step)[1:3])
                wait_recv(s_copies(step)[4:])

        compute(g * 8, rest)
        for step in range(groups):

            @pl.when(turn_of == 2 * step)
            def _(step=step):
                run(LATER[step])

    for g in range(groups):
        for one in results(8 * g):
            one.wait()
        wait_send(z_copies(g))
        wait_send(proxy_copies(g))
        wait_send(y_copies(g, 0))
        wait_send(y_copies(g, 1))
        wait_send(s_copies(g))


def halo(velocity, rows, cols):
    nt = velocity.shape[-1] // 128
    groups = nt // 8
    f32 = functools.partial(jax.ShapeDtypeStruct, dtype=jnp.float32)
    in_hbm = pl.BlockSpec(memory_space=pl.ANY)
    dma = pltpu.SemaphoreType.DMA
    scratch = lambda *shape: pltpu.VMEM((*shape, 128), jnp.float32)
    return pl.pallas_call(
        functools.partial(halo_kernel, rows, cols, nt),
        out_shape=(f32((12, DZ, nt * DY, 128)), f32((3, DZ + 2, 2, nt * DY, 128)), f32((6, DZ, DY, nt * 128))),
        in_specs=[in_hbm],
        out_specs=(in_hbm, in_hbm, in_hbm),
        scratch_shapes=[
            pltpu.VMEM(velocity.shape, jnp.float32),
            scratch(3, EZ, EY, nt + 16),
            scratch(6, EZ - 2, 8),
            scratch(6, DZ, (EY - 2) * 8),
            scratch(6, 8 * DY),
            scratch(12, DZ, EY - 2, 8),
            scratch(3, DZ + 2, EY, 8),
            scratch(12, DZ, nt * DY),
            scratch(3, DZ + 2, 2, nt * DY),
            pltpu.VMEM((6, DZ, DY, nt * 128), jnp.float32),
            dma((groups, 4)),
            dma((groups, 4)),
            dma((groups, 2, 2)),
            dma((groups, 2, 2)),
            dma((groups, 6)),
            dma((groups, 6)),
            dma((groups, 3)),
            dma,
        ],
        compiler_params=pltpu.CompilerParams(collective_id=0, has_side_effects=True, vmem_limit_bytes=VMEM_LIMIT),
        name="halo",
    )(velocity)


def band_matrix():
    taps = np.array([1, 2, 3, 4, 5, 4, 3, 2, 1], np.float32)
    center = np.zeros((128, 128), np.float32)
    edge = np.zeros((128, 128), np.float32)
    for source in range(128):
        for k in range(9):
            target = source + k - 4
            if 0 <= target < 128:
                center[source, target] = taps[k]
            else:
                edge[source, target % 128] = taps[k]
    half = np.concatenate([center, edge], axis=1)
    return np.concatenate([half, half], axis=0)


SCALE = 1.0 / 15625.0


def x_filter(flat, band, scale):
    high = flat.astype(jnp.bfloat16)
    low = (flat - high.astype(jnp.float32)).astype(jnp.bfloat16)
    both = jnp.dot(jnp.concatenate([high, low], axis=1), band, preferred_element_type=jnp.float32)
    center, edge = both[:, :128], both[:, 128:]
    lane = lax.broadcasted_iota(jnp.int32, flat.shape, 1)
    from_low = jnp.concatenate([edge[-DY:], edge[:-DY]], axis=0)
    from_high = jnp.concatenate([edge[DY:], edge[:DY]], axis=0)
    return (center + jnp.where(lane < 64, from_low, from_high)) * scale


def finish_kernel(rows, cols, nt, band, fp, fv, leonard, model, sums, bar, filtered):
    s = pl.program_id(0)
    shape = (DY, 128)
    lane = lax.broadcasted_iota(jnp.int32, shape, 1)
    line = lax.broadcasted_iota(jnp.int32, shape, 0)

    @pl.when(s == 0)
    def _():
        sums[...] = jnp.zeros_like(sums)

    r, c = lax.axis_index("row"), lax.axis_index("col")
    outside = jnp.logical_or(jnp.logical_and(s == 0, c == 0), jnp.logical_and(s == DZ + 1, c == cols - 1))
    keep = jnp.where(outside, 0.0, SCALE)
    for i in range(3):
        bar[i, s, 0] = x_filter(fv[i, 0, 0], band[...], keep)

    @pl.when(jnp.logical_and(s >= 1, s <= DZ))
    def _():
        below, above = jnp.where(r < rows - 1, 1.0, 0.0), jnp.where(r > 0, 1.0, 0.0)
        beyond = jnp.where(lax.broadcasted_iota(jnp.int32, (nt, DY, 128), 1) == 0, below, above).reshape(nt * DY, 128)
        for i in range(3):
            bar[i, s, 1] = x_filter(fv[i, 0, 1], band[...], SCALE) * beyond

    @pl.when(s >= 2)
    def _():
        k = s - 1

        for n in range(12):
            filtered[n] = x_filter(fp[n, 0], band[...], SCALE)

        @pl.loop(0, nt, step=32, init_carry=(jnp.zeros(shape, jnp.float32),) * 2)
        def totals(x0, carry):
            numer, denom = carry
            for x in range(32):
                x = x0 + x
                before, after = lax.rem(x + nt - 1, nt), lax.rem(x + 1, nt)
                at = lambda i, plane, x, part=0: bar[i, plane, part, pl.ds(pl.multiple_of(x * DY, DY), DY), :]
                u = [at(i, k, x) for i in range(3)]
                grads = []
                for i in range(3):
                    right = pltpu.roll(jnp.where(lane == 0, at(i, k, after), u[i]), 127, 1)
                    left = pltpu.roll(jnp.where(lane == 127, at(i, k, before), u[i]), 1, 1)
                    rim = at(i, k, x, 1)
                    down = pltpu.roll(jnp.where(line == 0, rim, u[i]), DY - 1, 0)
                    up = pltpu.roll(jnp.where(line == DY - 1, rim, u[i]), 1, 0)
                    grads.append([right - left, down - up, at(i, k + 1, x) - at(i, k - 1, x)])
                strain, quarter = strain_scaled(grads)
                scaled = 8.0 * quarter
                here = pl.ds(pl.multiple_of(x * DY, DY), DY)
                lanes = pl.ds(pl.multiple_of(x * 128, 128), 128)
                for n, (i, j) in enumerate(pair_list):
                    leonard_p = filtered[n, here, :] - u[i] * u[j]
                    model_p = 2.0 * filtered[6 + n, here, :] - scaled * strain[n]
                    leonard[n, 0, :, lanes] = leonard_p
                    model[n, 0, :, lanes] = model_p
                    weighted = model_p if pair_weight[n] == 1.0 else 2.0 * model_p
                    numer = numer + weighted * leonard_p
                    denom = denom + weighted * model_p
            return numer, denom

        sums[0] += totals[0]
        sums[1] += totals[1]


def finish(fp, fv, rows, cols, width):
    nt = width // 128
    f32 = functools.partial(jax.ShapeDtypeStruct, dtype=jnp.float32)
    scratch = lambda *shape: pltpu.VMEM((*shape, 128), jnp.float32)
    plane = lambda s: (0, jnp.maximum(s - 2, 0), 0, 0)
    return pl.pallas_call(
        functools.partial(finish_kernel, rows, cols, nt),
        grid=(DZ + 2,),
        out_shape=(f32((6, DZ, DY, width)), f32((6, DZ, DY, width)), f32((2, DY, 128))),
        in_specs=[
            pl.BlockSpec((256, 256), lambda s: (0, 0)),
            pl.BlockSpec((12, 1, nt * DY, 128), plane),
            pl.BlockSpec((3, 1, 2, nt * DY, 128), lambda s: (0, s, 0, 0, 0)),
        ],
        out_specs=(
            pl.BlockSpec((6, 1, DY, width), plane),
            pl.BlockSpec((6, 1, DY, width), plane),
            pl.BlockSpec((2, DY, 128), lambda s: (0, 0, 0)),
        ),
        scratch_shapes=[scratch(3, DZ + 2, 2, nt * DY), scratch(12, nt * DY)],
        compiler_params=pltpu.CompilerParams(vmem_limit_bytes=VMEM_LIMIT),
        name="finish",
    )(jnp.asarray(band_matrix(), jnp.bfloat16), fp, fv)


def total_kernel(cols, points, sums, coeff, own, parts, own_sem, send, recv):
    r = lax.axis_index("row")
    c = lax.axis_index("col")
    load = pltpu.make_async_copy(sums, own, own_sem)
    load.start()
    barrier = pltpu.get_barrier_semaphore()
    for step in range(1, cols):
        pl.semaphore_signal(barrier, inc=1, device_id=(r, lax.rem(c + step, cols)), device_id_type=MESH)
    pl.semaphore_wait(barrier, cols - 1)
    copies = [
        pltpu.make_async_remote_copy(
            src_ref=sums,
            dst_ref=parts.at[step - 1],
            send_sem=send.at[step - 1],
            recv_sem=recv.at[step - 1],
            device_id=(r, lax.rem(c + step, cols)),
            device_id_type=MESH,
        )
        for step in range(1, cols)
    ]
    for one in copies:
        one.start()
    load.wait()
    added = own[...]
    for step, one in enumerate(copies):
        one.wait_recv()
        added = added + parts[step]
    numer = jnp.sum(added[0], axis=1, keepdims=True) / points
    denom = jnp.sum(added[1], axis=1, keepdims=True) / points
    ratio = jnp.maximum(numer / (denom + 1e-06), 0.0)
    coeff[...] = jnp.broadcast_to(-2.0 * ratio, coeff.shape)
    for one in copies:
        one.wait_send()


def total(sums, cols, width):
    in_vmem = pl.BlockSpec(memory_space=VMEM)
    dma = pltpu.SemaphoreType.DMA
    return pl.pallas_call(
        functools.partial(total_kernel, cols, width * DZ * cols),
        out_shape=jax.ShapeDtypeStruct((DY, width), jnp.float32),
        in_specs=[pl.BlockSpec(memory_space=pl.ANY)],
        out_specs=in_vmem,
        scratch_shapes=[pltpu.VMEM((2, DY, 128), jnp.float32), pltpu.VMEM((cols - 1, 2, DY, 128), jnp.float32), dma, dma((cols - 1,)), dma((cols - 1,))],
        compiler_params=pltpu.CompilerParams(collective_id=1, has_side_effects=True),
        name="total",
    )(sums)


def on_device(velocity):
    rows, cols = lax.axis_size("row"), lax.axis_size("col")
    width = velocity.shape[-1]
    fp, fv, ms = halo(velocity, rows, cols)
    leonard, model, sums = finish(fp, fv, rows, cols, width)
    coeff = total(sums, cols, width)
    return leonard, model, ms * coeff[None, None]


def solution(mesh):
    placed = P(None, "col", "row", None)
    return jax.shard_map(on_device, mesh=mesh, in_specs=(placed,), out_specs=(placed, placed, placed), check_vma=False)
```
